512 devices in a mesh: branch: 64 (over z, y), sub: 8 (over x, core).
Axes of the slice: x: 4, y: 8, z: 8, core: 2. Of those that a mesh axis runs over, the one named last changes fastest.
Arguments:
- vectors: float32 [64, 2097152], P(None, ('branch', 'sub')), may hold values from -1.6 to 1.6
- coords: float32 [2, 2097152], P(None, ('branch', 'sub')), may hold values from 0 to 3
- basis: float32 [32, 2097152], P(None, ('branch', 'sub')), may hold values from -0.5 to 0.5
- leaf_transfer: float32 [16384, 32, 32], P(('branch', 'sub')), may hold values from -1 to 1
- node_transfer: float32 [512, 32, 32], P(('branch', 'sub')), may hold values from -0.375 to 0.375
- skel_one: float32 [512, 2, 32], P(('branch', 'sub')), may hold values from 0 to 3
- skel_two: float32 [64, 2, 32], replicated, may hold values from 0 to 3
- near_list: int32 [16384, 9], P(('branch', 'sub')), may hold values from 0 to 16383, as said below
- list_one: int32 [512, 8], P(('branch', 'sub')), may hold values from 0 to 511, as said below
- list_two: int32 [64, 8], P('branch'), may hold values from 0 to 63
Outputs:
- product: float32 [64, 2097152], P(None, ('branch', 'sub'))
The draws below stay inside these ranges and needn't reach their ends.
Inputs may be any that keep to these rules, and one draw needn't show every extreme that they name: `near_list`: entry 0 of each row is the leaf itself. Every entry names a leaf of the same sub-branch, or of the sub-branch one branch index lower or higher with the same sub index (the leaf numbered (b * 8 + s) * 32 + i lies in branch group b, sub-branch s); those of the lower one are among its last 8 leaves, those of the higher one among its first 8, and in every draw some leaf names the first of those last 8 and some the last of those first 8. `list_one`: node n = b * 8 + s names only nodes with the same sub index s.
All inputs are finite; a program needn't handle non-finite values.
Results may differ from the reference program's by a relative error of at most 0.00015.
Values sent between devices are 32-bit elements; how exact they have to be, the bound alone decides.
A program may use at most 64 MiB of HBM per device.

```python
import jax
import jax.numpy as jnp
from jax import lax

LEAF = 128
RANK = 32
NV = 64
LEAF_DEV = 32
NEAR = 9
K1 = 8
K2 = 8
RIM = 8
GROUPS = 64
SUBS = 8
NODES = 512
LEAVES = 16384
POINTS = 2097152


def draw_near_list(key, part):
    key = jax.random.fold_in(key, 11)
    leaf_ids = jnp.arange(LEAVES, dtype=jnp.int32)[:, None]
    device_ids = leaf_ids // LEAF_DEV
    local_ids = leaf_ids % LEAF_DEV
    group_ids = device_ids // SUBS
    columns = jnp.arange(NEAR, dtype=jnp.int32)[None, :]
    choose = jax.random.randint(key, (LEAVES, NEAR), 0, LEAF_DEV + 2 * RIM, dtype=jnp.int32)
    choose = jnp.where(columns == 0, RIM + local_ids, choose)
    choose = jnp.where((columns == 1) & (local_ids == 0), 0, choose)
    choose = jnp.where((columns == 2) & (local_ids == LEAF_DEV - 1), LEAF_DEV + 2 * RIM - 1, choose)
    offset = jnp.where(choose < RIM, -1, jnp.where(choose < RIM + LEAF_DEV, 0, 1))
    source_local = jnp.where(offset < 0, LEAF_DEV - RIM + choose, jnp.where(offset == 0, choose - RIM, choose - RIM - LEAF_DEV))
    valid = (group_ids + offset >= 0) & (group_ids + offset < GROUPS)
    offset = jnp.where(valid, offset, 0)
    source_local = jnp.where(valid, source_local, local_ids)
    return ((device_ids + offset * SUBS) * LEAF_DEV + source_local).astype(jnp.int32)


def draw_list_one(key, part):
    key = jax.random.fold_in(key, 23)
    node_ids = jnp.arange(NODES, dtype=jnp.int32)[:, None]
    branches = jax.random.randint(key, (NODES, K1), 0, GROUPS, dtype=jnp.int32)
    return (branches * SUBS + node_ids % SUBS).astype(jnp.int32)


def place_ends(drawn, own_key, least, largest):
    extent = drawn.shape
    place = [jax.random.randint(jax.random.fold_in(own_key, axis), (), 0, extent[axis]) for axis in range(len(extent))]
    drawn = drawn.at[tuple(place)].set(least)
    longest = extent.index(max(extent))
    place[longest] = (place[longest] + 1) % extent[longest]
    return drawn.at[tuple(place)].set(largest)


def levels(own_key, extent, pieces, low, largest):
    loudness, own = 1.0, jax.random.fold_in(own_key, 6)
    for axis_at, parts in pieces:
        heights = jnp.exp(jax.random.uniform(jax.random.fold_in(own, axis_at), (parts,), jnp.float32, low / len(pieces), largest / len(pieces)))
        loudness = loudness * jnp.repeat(heights, extent[axis_at] // parts).reshape([-1 if axis == axis_at else 1 for axis in range(len(extent))])
    return loudness


def scatter_about(rng, dims, spread, limit, shards=(), kind=jnp.bfloat16):
    factor_of = levels(rng, dims, shards, -0.22, 0.18) if shards else 1.0
    result = jax.random.normal(rng, dims, jnp.float32) * spread * factor_of
    return jnp.minimum(jnp.maximum(result, -limit), limit).astype(kind)


def setup_inputs(seed: int = 0) -> dict:
    key_of = jax.random.split(jax.random.key(seed), 11)
    return {
        "vectors": scatter_about(key_of[0], (NV, POINTS), 0.2, 1.6, ((1, 512),), jnp.float32),
        "coords": jnp.clip(3.0 * jax.random.uniform(key_of[1], (2, POINTS), jnp.float32) ** levels(key_of[1], (2, POINTS), ((1, 512),), -0.2, 0.2), 0.0, 3.0),
        "basis": scatter_about(key_of[2], (RANK, POINTS), LEAF ** -0.5, 0.5, ((1, 512),), jnp.float32),
        "leaf_transfer": scatter_about(key_of[3], (LEAVES, RANK, RANK), RANK ** -0.5, 1.0, ((0, 512),), jnp.float32),
        "node_transfer": scatter_about(key_of[4], (NODES, RANK, RANK), (RANK * SUBS) ** -0.5, 0.375, ((0, 512),), jnp.float32),
        "skel_one": jnp.clip(3.0 * jax.random.uniform(key_of[5], (NODES, 2, RANK), jnp.float32) ** levels(key_of[5], (NODES, 2, RANK), ((0, 512),), -0.2, 0.2), 0.0, 3.0),
        "skel_two": jnp.clip(jax.random.uniform(key_of[6], (GROUPS, 2, RANK), jnp.float32, 0.0, 3.0), 0.0, 3.0),
        "near_list": draw_near_list(jax.random.fold_in(key_of[10], 71), 0),
        "list_one": draw_list_one(jax.random.fold_in(key_of[10], 71), 0),
        "list_two": place_ends(jax.random.randint(key_of[9], (GROUPS, K2), 0, GROUPS), jax.random.fold_in(key_of[9], 1), 0, GROUPS - 1).astype(jnp.int32),
    }


NUGGET = 0.5
LENGTH_SCALE = 0.7
ROOT_THREE = 1.7320508075688772

def matern(target, source):
    delta_x = target[..., 0, :, None] - source[..., 0, None, :]
    delta_y = target[..., 1, :, None] - source[..., 1, None, :]
    distance = jnp.sqrt(delta_x * delta_x + delta_y * delta_y)
    scaled = ROOT_THREE / LENGTH_SCALE * distance
    return (1.0 + scaled) * jnp.exp(-scaled)

def reference(vectors, coords, basis, leaf_transfer, node_transfer, skel_one, skel_two, near_list, list_one, list_two):
    precise = lax.Precision.HIGHEST
    vec_count = vectors.shape[0]
    leaf_vecs = vectors.reshape(vec_count, LEAVES, LEAF)
    leaf_points = jnp.transpose(coords.reshape(2, LEAVES, LEAF), (1, 0, 2))
    leaf_basis = basis.reshape(RANK, LEAVES, LEAF)
    coeff_leaf = jnp.einsum('rlp,vlp->lrv', leaf_basis, leaf_vecs, precision=precise)
    moved = jnp.einsum('lqr,lqv->lrv', leaf_transfer, coeff_leaf, precision=precise)
    coeff_node = moved.reshape(NODES, LEAF_DEV, RANK, vec_count).sum(1)
    upward = jnp.einsum('nqr,nqv->nrv', node_transfer, coeff_node, precision=precise)
    coeff_group = upward.reshape(GROUPS, SUBS, RANK, vec_count).sum(1)
    tile_two = matern(skel_two[:, None], skel_two[list_two])
    field_group = jnp.einsum('gkij,gkjv->giv', tile_two, coeff_group[list_two], precision=precise)
    tile_one = matern(skel_one[:, None], skel_one[list_one])
    field_node = jnp.einsum('nkij,nkjv->niv', tile_one, coeff_node[list_one], precision=precise)
    parent_field = jnp.repeat(field_group, SUBS, axis=0)
    field_node = field_node + jnp.einsum('nrq,nqv->nrv', node_transfer, parent_field, precision=precise)
    node_field = jnp.repeat(field_node, LEAF_DEV, axis=0)
    field_leaf = jnp.einsum('lrq,lqv->lrv', leaf_transfer, node_field, precision=precise)
    far_part = jnp.einsum('rlp,lrv->vlp', leaf_basis, field_leaf, precision=precise)
    block_leaves = min(64, LEAVES)

    def near_block(block_start):
        chosen = lax.dynamic_slice_in_dim(near_list, block_start, block_leaves, 0)
        target = lax.dynamic_slice_in_dim(leaf_points, block_start, block_leaves, 0)
        source = leaf_points[chosen]
        source_vecs = leaf_vecs[:, chosen]
        kernel_tile = matern(target[:, None], source)
        return jnp.einsum('bjpq,vbjq->vbp', kernel_tile, source_vecs, precision=precise)
    starts = jnp.arange(LEAVES // block_leaves, dtype=jnp.int32) * block_leaves
    near_part = lax.map(near_block, starts)
    near_part = jnp.transpose(near_part, (1, 0, 2, 3)).reshape(vec_count, LEAVES, LEAF)
    product = near_part + far_part + NUGGET * leaf_vecs
    return product.reshape(vec_count, POINTS)
```

```python
import functools
import math

import jax
import jax.numpy as jnp
from jax import lax
from jax.experimental import pallas as pl
from jax.experimental.pallas import tpu as pltpu
from jax.sharding import PartitionSpec as P

MESH = pl.DeviceIdType.MESH
F32 = jnp.float32
BF16 = jnp.bfloat16
NUGGET = 0.5
LOG2E = math.log2(math.e)
LN2 = math.log(2.0)
SCALE = math.sqrt(3.0) / 0.7 * LOG2E
Y_COUNT = 8
LEAF = 128
RANK = 32
NV = 64
RIM = 8
UNROLL = 4
PAIRS = ((0, 1), (2, 3), (4, 5), (6, 7), (8,))
EXACT = lax.Precision.HIGHEST


def split(x):
    high = x.astype(BF16)
    return high, (x - high.astype(F32)).astype(BF16)


def matern_scaled(sx, sy, tx, ty):
    dx = sx - tx
    dy = sy - ty
    square = jnp.maximum(dx * dx + dy * dy, 1e-30)
    dist = square * lax.rsqrt(square)
    return (dist + LOG2E) * jnp.exp2(-dist)


def dot_f32(a, b, dims=((1,), (0,))):
    return lax.dot_general(a, b, (dims, ((), ())), precision=EXACT, preferred_element_type=F32)


def dot_bf16(a, b, dims=((1,), (0,))):
    return lax.dot_general(a, b, (dims, ((), ())), preferred_element_type=F32)


def fold(r):
    half = r.shape[0] // 2, r.shape[1] // 2
    return r[: half[0], : half[1]] + r[half[0] :, : half[1]] + r[: half[0], half[1] :] + r[half[0] :, half[1] :]


def leaf_cols(i):
    return pl.ds(pl.multiple_of(i * LEAF, LEAF), LEAF)


def kernel(
    sizes, vec, crd, bas, ltr, ntr, sk1, sk2, near, list1, list2, out,
    hv, hc, vw, sbx, sby, w3, g0, g1, gg, ps, ru, fc, send, recv,
):
    n_branch, n_sub, n_y = sizes
    n_z = n_branch // n_y
    leaves = ltr.shape[0]
    rows = 16 // n_sub
    b = lax.axis_index("branch")
    s = lax.axis_index("sub")
    z = b // n_y
    y = b % n_y
    lower = (b + n_branch - 1) % n_branch
    upper = (b + 1) % n_branch

    def y_peer(d):
        return z * n_y + (y + d) % n_y, s

    def z_peer(d):
        return ((z + d) % n_z) * n_y + y, s

    def sub_peer(d):
        return b, (s + d) % n_sub

    def remote(src, dst, k, peer):
        return pltpu.make_async_remote_copy(
            src_ref=src, dst_ref=dst, send_sem=send.at[k], recv_sem=recv.at[k], device_id=peer, device_id_type=MESH
        )

    ys, zs, ss = range(1, n_y), range(1, n_z), range(1, n_sub)
    barrier = pltpu.get_barrier_semaphore()
    peers = [sub_peer(d) for d in ss] + [y_peer(d) for d in ys] + [z_peer(d) for d in zs] + [(lower, s), (upper, s)]
    for peer in peers:
        pl.semaphore_signal(barrier, inc=1, device_id=peer, device_id_type=MESH)

    def own_vectors(i, c):
        high, low = split(vec[:, leaf_cols(i)] * LN2)
        vw[RIM + i, :NV] = high
        vw[RIM + i, NV:] = low
        return c

    lax.fori_loop(0, leaves, own_vectors, 0, unroll=4)
    pl.semaphore_wait(barrier, len(peers))

    rim = RIM * LEAF
    first, last = pl.ds(0, rim), pl.ds(leaves * LEAF - rim, rim)
    halo = [
        remote(crd.at[:, first], hc.at[1], 0, (lower, s)),
        remote(crd.at[:, last], hc.at[0], 1, (upper, s)),
        remote(vec.at[:, first], hv.at[1], 2, (lower, s)),
        remote(vec.at[:, last], hv.at[0], 3, (upper, s)),
    ]
    for copy in halo:
        copy.start()

    def make_w(i, c):
        cols = leaf_cols(i)
        bh, bl = split(bas[:, cols])
        lh, ll = split(ltr[i].T)
        w = dot_bf16(jnp.concatenate([lh, lh, ll], 1), jnp.concatenate([bh, bl, bh], 0))
        wh, wl = split(w)
        w3[:RANK, cols] = wh
        w3[RANK : 2 * RANK, cols] = wl
        w3[2 * RANK :, cols] = wh
        return c

    lax.fori_loop(0, leaves, make_w, 0, unroll=4)

    def up(i, c):
        return c + dot_bf16(vw[RIM + i], w3[: 2 * RANK, leaf_cols(i)], ((1,), (1,)))

    coeff_t = fold(lax.fori_loop(0, leaves, up, jnp.zeros((2 * NV, 2 * RANK), F32), unroll=4)) * (1.0 / LN2)
    up_t = dot_f32(coeff_t, ntr[0])
    packed = jnp.concatenate([up_t[16 * k : 16 * (k + 1)] for k in range(4)], 1)
    for p in range(n_sub):
        ps[p] = packed[p * rows : (p + 1) * rows]
    for d in ss:
        remote(ps.at[(s + d) % n_sub], ru.at[d], 8, sub_peer(d)).start()

    coeff = coeff_t.T
    g0[0, 0] = jnp.concatenate([coeff[0:8], coeff[8:16]], 1)
    g1[0, 0] = jnp.concatenate([coeff[16:24], coeff[24:32]], 1)
    gg[0, 0, rows : rows + 1] = jnp.concatenate([sk1[0, 0:1], sk1[0, 1:2], jnp.zeros((1, 2 * RANK), F32)], 1)
    for d in ys:
        remote(g0.at[0, 0], g0.at[0, d], 4, y_peer(d)).start()
    for d in zs:
        remote(g1.at[0, 0], g1.at[0, d], 5, z_peer(d)).start()

    def place_coords(i, row_x, row_y):
        sbx[i] = jnp.broadcast_to(row_x * SCALE, (LEAF, LEAF)).T
        sby[i] = jnp.broadcast_to(row_y * SCALE, (LEAF, LEAF)).T

    def own_coords(i, c):
        place_coords(RIM + i, crd[0:1, leaf_cols(i)], crd[1:2, leaf_cols(i)])
        return c

    lax.fori_loop(0, leaves, own_coords, 0, unroll=2)

    remote(ru.at[pl.ds(1, n_sub - 1)], ru.at[pl.ds(1, n_sub - 1)], 8, sub_peer(1)).wait_recv()
    total = ps[s]
    for d in ss:
        total = total + ru[d]
    gg[0, 0, 0:rows] = total
    for d in ys:
        remote(gg.at[0, 0], gg.at[0, d], 9, y_peer(d)).start()

    for copy in halo[:2]:
        copy.wait_recv()
    for side in range(2):
        base = side * (RIM + leaves)

        def rim_coords(i, c, side=side, base=base):
            place_coords(base + i, hc[side, 0:1, leaf_cols(i)], hc[side, 1:2, leaf_cols(i)])
            return c

        lax.fori_loop(0, RIM, rim_coords, 0, unroll=2)
    for copy in halo[2:]:
        copy.wait_recv()
    for side in range(2):
        base = side * (RIM + leaves)

        def rim_vectors(i, c, side=side, base=base):
            high, low = split(hv[side, :, leaf_cols(i)] * LN2)
            vw[base + i, :NV] = high
            vw[base + i, NV:] = low
            return c

        lax.fori_loop(0, RIM, rim_vectors, 0, unroll=4)

    def near_leaf(i):
        cols = leaf_cols(i)
        tx, ty = crd[0:1, cols] * SCALE, crd[1:2, cols] * SCALE
        slots = []
        for j in range(9):
            named = near[i, j]
            slot = (named // (n_sub * leaves) - b) * leaves + named % leaves + RIM
            slots.append(jnp.clip(slot, 0, leaves + 2 * RIM - 1))
        acc = None
        for pair in PAIRS:
            tiles = [
                jnp.concatenate(split(matern_scaled(sbx[slots[j]], sby[slots[j]], tx, ty)), 1) for j in pair
            ]
            part = dot_bf16(jnp.concatenate([vw[slots[j]] for j in pair], 1), jnp.concatenate(tiles, 0))
            acc = part if acc is None else acc + part
        out[:, cols] = fold(acc) + NUGGET * vec[:, cols]

    def forward():
        remote(gg.at[0, pl.ds(1, n_y - 1)], gg.at[0, pl.ds(1, n_y - 1)], 9, y_peer(1)).wait_recv()
        for d in zs:
            remote(gg.at[0], gg.at[d], 10, z_peer(d)).start()
        remote(g0.at[0, pl.ds(1, n_y - 1)], g0.at[0, pl.ds(1, n_y - 1)], 4, y_peer(1)).wait_recv()
        for d in zs:
            remote(g0.at[0], g0.at[d], 6, z_peer(d)).start()
        remote(g1.at[0, pl.ds(1, n_z - 1)], g1.at[0, pl.ds(1, n_z - 1)], 5, z_peer(1)).wait_recv()
        for d in ys:
            remote(g1.at[0], g1.at[d], 7, y_peer(d)).start()

    def place_of(branch):
        return (z + n_z - branch // n_y) % n_z, (y + n_y - branch % n_y) % n_y

    def far_tile(target, sources):
        column = (target * SCALE).T
        sx = jnp.concatenate([a for a, _ in sources], 1) * SCALE
        sy = jnp.concatenate([c for _, c in sources], 1) * SCALE
        wide = (RANK, sx.shape[1])
        return matern_scaled(
            jnp.broadcast_to(sx, wide), jnp.broadcast_to(sy, wide),
            jnp.broadcast_to(column[:, 0:1], wide), jnp.broadcast_to(column[:, 1:2], wide),
        ) * LN2

    def group_field():
        remote(gg.at[pl.ds(1, n_z - 1)], gg.at[pl.ds(1, n_z - 1)], 10, z_peer(1)).wait_recv()
        sources, coeffs = [], []
        for k in range(8):
            m = list2[0, k]
            dz, dy = place_of(m)
            skel = sk2[m]
            sources.append((skel[0:1], skel[1:2]))
            block = gg[dz, dy][0:rows]
            coeffs.append(jnp.concatenate([block[:, RANK * q : RANK * (q + 1)] for q in range(4)], 0))
        field = dot_f32(jnp.concatenate(coeffs, 1), far_tile(sk2[b], sources), ((1,), (1,)))
        fc[0] = jnp.concatenate([field[rows * q : rows * (q + 1)] for q in range(4)], 1)
        for d in ss:
            remote(fc.at[0], fc.at[d], 11, sub_peer(d)).start()

    def near_block(t, c):
        for u in range(UNROLL):
            near_leaf(t * UNROLL + u)

        @pl.when(t == 0)
        def _():
            forward()

        @pl.when(t == 2)
        def _():
            group_field()

        return c

    lax.fori_loop(0, leaves // UNROLL, near_block, 0)

    remote(g0.at[pl.ds(1, n_z - 1)], g0.at[pl.ds(1, n_z - 1)], 6, z_peer(1)).wait_recv()
    remote(g1.at[pl.ds(1, n_y - 1)], g1.at[pl.ds(1, n_y - 1)], 7, y_peer(1)).wait_recv()
    sources, coeffs = [], []
    for k in range(8):
        dz, dy = place_of(list1[0, k] // n_sub)
        skel = gg[dz, dy][rows : rows + 1]
        sources.append((skel[:, 0:RANK], skel[:, RANK : 2 * RANK]))
        for block in (g0[dz, dy], g1[dy, dz]):
            coeffs += [block[:, :NV], block[:, NV:]]
    field = dot_f32(far_tile(sk1[0], sources), jnp.concatenate(coeffs, 0))
    remote(fc.at[pl.ds(1, n_sub - 1)], fc.at[pl.ds(1, n_sub - 1)], 11, sub_peer(1)).wait_recv()
    packed = jnp.concatenate([fc[(s + n_sub - p) % n_sub] for p in range(n_sub)], 0)
    group_t = jnp.concatenate([packed[:, RANK * q : RANK * (q + 1)] for q in range(4)], 0)
    field = field + dot_f32(ntr[0], group_t, ((1,), (1,)))
    fh, fl = split(field.T)
    lhs = jnp.concatenate([fh, fh, fl], 1)

    def far(i, c):
        cols = pl.ds(pl.multiple_of(i * 2 * LEAF, 2 * LEAF), 2 * LEAF)
        out[:, cols] += dot_bf16(lhs, w3[:, cols])
        return c

    lax.fori_loop(0, leaves // 2, far, 0, unroll=4)

    for copy in halo:
        copy.wait_send()
    ny1, nz1, ns1 = pl.ds(1, n_y - 1), pl.ds(1, n_z - 1), pl.ds(1, n_sub - 1)
    for ref, k in (
        (g0.at[0, ny1], 4), (g1.at[0, nz1], 5), (g0.at[nz1], 6), (g1.at[ny1], 7),
        (ru.at[ns1], 8), (gg.at[0, ny1], 9), (gg.at[nz1], 10), (fc.at[ns1], 11),
    ):
        remote(ref, ref, k, sub_peer(1)).wait_send()


def body(sizes, vectors, coords, basis, leaf_transfer, node_transfer, skel_one, skel_two, near_list, list_one, list_two):
    n_branch, n_sub, n_y = sizes
    n_z = n_branch // n_y
    leaves = leaf_transfer.shape[0]
    window = leaves + 2 * RIM
    rows = 16 // n_sub
    rim = RIM * LEAF
    vmem = pl.BlockSpec(memory_space=pltpu.VMEM)
    smem = pl.BlockSpec(memory_space=pltpu.SMEM)
    return pl.pallas_call(
        functools.partial(kernel, sizes),
        out_shape=jax.ShapeDtypeStruct(vectors.shape, F32),
        in_specs=[vmem] * 7 + [smem] * 3,
        out_specs=vmem,
        scratch_shapes=[
            pltpu.VMEM((2, NV, rim), F32),
            pltpu.VMEM((2, 2, rim), F32),
            pltpu.VMEM((window, 2 * NV, LEAF), BF16),
            pltpu.VMEM((window, LEAF, LEAF), F32),
            pltpu.VMEM((window, LEAF, LEAF), F32),
            pltpu.VMEM((3 * RANK, leaves * LEAF), BF16),
            pltpu.VMEM((n_z, n_y, 8, 128), F32),
            pltpu.VMEM((n_y, n_z, 8, 128), F32),
            pltpu.VMEM((n_z, n_y, 2 * rows, 128), F32),
            pltpu.VMEM((n_sub, rows, 128), F32),
            pltpu.VMEM((n_sub, rows, 128), F32),
            pltpu.VMEM((n_sub, rows, 128), F32),
            pltpu.SemaphoreType.DMA((12,)),
            pltpu.SemaphoreType.DMA((12,)),
        ],
        compiler_params=pltpu.CompilerParams(
            collective_id=0, has_side_effects=True, vmem_limit_bytes=48 * 2**20
        ),
        name="h2_product",
    )(vectors, coords, basis, leaf_transfer, node_transfer, skel_one, skel_two, near_list, list_one, list_two)


def solution(mesh, y_count=Y_COUNT):
    both = ("branch", "sub")
    return jax.shard_map(
        functools.partial(body, (mesh.shape["branch"], mesh.shape["sub"], y_count)),
        mesh=mesh,
        in_specs=(
            P(None, both),
            P(None, both),
            P(None, both),
            P(both, None, None),
            P(both, None, None),
            P(both, None, None),
            P(),
            P(both, None),
            P(both, None),
            P("branch", None),
        ),
        out_specs=P(None, both),
        check_vma=False,
    )
```

```python
import functools
import math

import jax
import jax.numpy as jnp
from jax import lax
from jax.experimental import pallas as pl
from jax.experimental.pallas import tpu as pltpu
from jax.sharding import PartitionSpec as P

MESH = pl.DeviceIdType.MESH
F32 = jnp.float32
BF16 = jnp.bfloat16
NUGGET = 0.5
LOG2E = math.log2(math.e)
LN2 = math.log(2.0)
SCALE = math.sqrt(3.0) / 0.7 * LOG2E
Y_COUNT = 8
LEAF = 128
RANK = 32
NV = 64
RIM = 8
BLOCK = 8
PAIRS = ((0, 1), (2, 3), (4, 5), (6, 7), (8,))
EXACT = lax.Precision.HIGHEST
CENTRE = 1.5
VMEM_LIMIT = 62 * 2**20
FEATURES = 32
NN, NT, TN = ((1,), (0,)), ((1,), (1,)), ((0,), (0,))


def split(x):
    high = x.astype(BF16)
    return high, (x - high.astype(F32)).astype(BF16)


def split3(x):
    first = x.astype(BF16).astype(F32)
    rest = x - first
    second = rest.astype(BF16).astype(F32)
    return first, second, rest - second


def matern_of(square):
    square = jnp.maximum(square, 1e-30)
    dist = square * lax.rsqrt(square)
    return (dist + LOG2E) * jnp.exp2(-dist)


def features(coords):
    w = (coords - CENTRE) * SCALE
    norm = w[0:1] * w[0:1] + w[1:2] * w[1:2]
    s1, s2, s3 = split3(w)
    norms = split3(norm)
    ones = [jnp.ones_like(norm)] * 3
    zeros = jnp.zeros((FEATURES - 18, w.shape[1]), F32)
    t1, t2, t3 = -2.0 * s1, -2.0 * s2, -2.0 * s3
    source = jnp.concatenate([s1, s1, s2, s2, s1, s3, *norms, *ones, zeros], 0)
    target = jnp.concatenate([t1, t2, t1, t2, t3, t1, *ones, *norms, zeros], 0)
    return source, target


def dot_f32(a, b, dims=NN):
    return lax.dot_general(a, b, (dims, ((), ())), precision=EXACT, preferred_element_type=F32)


def dot_bf16(a, b, dims=NN):
    return lax.dot_general(a, b, (dims, ((), ())), preferred_element_type=F32)


def fold(r):
    half = r.shape[0] // 2, r.shape[1] // 2
    return r[: half[0], : half[1]] + r[half[0] :, : half[1]] + r[: half[0], half[1] :] + r[half[0] :, half[1] :]


def leaf_cols(i):
    return pl.ds(pl.multiple_of(i * LEAF, LEAF), LEAF)


def kernel(sizes, *refs):
    operands, out = refs[:10], refs[10]
    vec, crd, bas, ltr, ntr, sk1, sk2, near, list1, list2 = refs[11:21]
    hv, hc, vw, fs, ft, w3, sk2t, gy, gz, gs, ps, ru, fc, load, send, recv, later = refs[21:]
    n_branch, n_sub, n_y = sizes
    n_z = n_branch // n_y
    leaves = ltr.shape[0]
    rows = 16 // n_sub
    ny1, nz1, ns1 = pl.ds(1, n_y - 1), pl.ds(1, n_z - 1), pl.ds(1, n_sub - 1)
    b = lax.axis_index("branch")
    s = lax.axis_index("sub")
    z = b // n_y
    y = b % n_y

    loads = [pltpu.make_async_copy(operands[k], refs[11 + k], load.at[k]) for k in range(10)]
    l_vec, l_crd, l_bas, l_ltr, l_ntr, l_sk1, l_sk2, l_near, l_list1, l_list2 = loads
    for copy in (l_ltr, l_bas, l_vec, l_crd, l_ntr, l_sk1, l_sk2, l_near, l_list1, l_list2):
        copy.start()

    def y_peer(d):
        return z * n_y + (y + d) % n_y, s

    def z_peer(d):
        return ((z + d) % n_z) * n_y + y, s

    def sub_peer(d):
        return b, (s + d) % n_sub

    def remote(src, dst, k, peer):
        return pltpu.make_async_remote_copy(
            src_ref=src, dst_ref=dst, send_sem=send.at[k], recv_sem=recv.at[k], device_id=peer, device_id_type=MESH
        )

    def signal(sem, peer):
        pl.semaphore_signal(sem, inc=1, device_id=peer, device_id_type=MESH)

    ys, zs, ss = range(1, n_y), range(1, n_z), range(1, n_sub)
    has_lower, has_upper = b > 0, b < n_branch - 1
    lower, upper = (b - 1, s), (b + 1, s)

    barrier = pltpu.get_barrier_semaphore()
    pl.when(has_lower)(lambda: signal(barrier, lower))
    pl.when(has_upper)(lambda: signal(barrier, upper))
    for d in ss:
        signal(barrier, sub_peer(d))
    for d in ys:
        signal(barrier, y_peer(d))
    for other in range(1, n_z):
        pl.when(other > z)(lambda other=other: signal(barrier, (other * n_y + y, s)))

    for side, missing in ((0, b == 0), (1, b == n_branch - 1)):

        @pl.when(missing)
        def _(side=side):
            hv[side] = jnp.zeros(hv.shape[1:], F32)
            hc[side] = jnp.zeros(hc.shape[1:], F32)

    l_ltr.wait()
    l_bas.wait()

    def make_w(i, c):
        cols = leaf_cols(i)
        bh, bl = split(bas[:, cols])
        lh, ll = split(ltr[i])
        w = dot_bf16(jnp.concatenate([lh, lh, ll], 0), jnp.concatenate([bh, bl, bh], 0), TN)
        wh, wl = split(w)
        w3[:RANK, cols] = wh
        w3[RANK : 2 * RANK, cols] = wl
        w3[2 * RANK :, cols] = wh
        return c

    lax.fori_loop(0, leaves, make_w, 0, unroll=16)

    l_vec.wait()

    def own_vectors(i, c):
        high, low = split(vec[:, leaf_cols(i)] * LN2)
        vw[RIM + i, :NV] = high
        vw[RIM + i, NV:] = low
        return c

    lax.fori_loop(0, leaves, own_vectors, 0, unroll=8)
    own = jnp.concatenate([vw[RIM + i] for i in range(leaves)], 1)
    coeff_t = fold(dot_bf16(own, w3[: 2 * RANK], NT)) * (1.0 / LN2)
    l_ntr.wait()
    up_t = dot_f32(coeff_t, ntr[0])
    packed = jnp.concatenate([up_t[16 * k : 16 * (k + 1)] for k in range(4)], 1)
    for p in range(n_sub):
        ps[p] = packed[p * rows : (p + 1) * rows]

    met = n_sub - 1 + n_y - 1 + z + has_lower.astype(jnp.int32) + has_upper.astype(jnp.int32)
    pl.semaphore_wait(barrier, met)
    for d in ss:
        remote(ps.at[(s + d) % n_sub], ru.at[d], 8, sub_peer(d)).start()
    for other in range(n_z - 1):
        pl.when(other < z)(lambda other=other: signal(later, (other * n_y + y, s)))

    rim = RIM * LEAF
    first, last = pl.ds(0, rim), pl.ds(leaves * LEAF - rim, rim)
    down = [remote(crd.at[:, first], hc.at[1], 0, lower), remote(vec.at[:, first], hv.at[1], 2, lower)]
    up = [remote(crd.at[:, last], hc.at[0], 1, upper), remote(vec.at[:, last], hv.at[0], 3, upper)]

    def start_all(copies):
        for copy in copies:
            copy.start()

    def send_halo():
        pl.when(has_lower)(lambda: start_all(down))
        pl.when(has_upper)(lambda: start_all(up))

    coeff = coeff_t.T
    coeff = jnp.concatenate([coeff[:16], coeff[16:]], 1)
    for k in range(3):
        gy[0, 0, k] = coeff[4 * k : 4 * (k + 1)]
    gz[0, 0] = coeff[12:16]
    for d in ys:
        remote(gy.at[0, 0], gy.at[0, d], 4, y_peer(d)).start()

    l_crd.wait()
    send_halo()
    wide = 8 * LEAF

    def own_features(i, c):
        cols = pl.ds(pl.multiple_of(i * wide, wide), wide)
        source, target = features(crd[:, cols])
        ft[:, cols] = target.astype(BF16)
        flat = source.T.astype(BF16)
        for k in range(8):
            fs[RIM + i * 8 + k] = flat[k * LEAF : (k + 1) * LEAF]
        return c

    lax.fori_loop(0, leaves // 8, own_features, 0)
    l_sk1.wait()
    gs[0, 0, rows : rows + 1] = jnp.concatenate([sk1[0, 0:1], sk1[0, 1:2], jnp.zeros((1, 2 * RANK), F32)], 1)

    remote(ru.at[ns1], ru.at[ns1], 8, sub_peer(1)).wait_recv()
    total = ps[s]
    for d in ss:
        total = total + ru[d]
    gs[0, 0, 0:rows] = total

    @pl.when(z < n_z - 1)
    def _():
        pl.semaphore_wait(later, n_z - 1 - z)

    for d in zs:
        remote(gs.at[0, 0], gs.at[0, d], 11, z_peer(d)).start()
    for d in zs:
        remote(gz.at[0, 0], gz.at[0, d], 5, z_peer(d)).start()

    def pass_on():
        remote(gs.at[0, nz1], gs.at[0, nz1], 11, z_peer(1)).wait_recv()
        for d in ys:
            remote(gs.at[0], gs.at[d], 7, y_peer(d)).start()
        remote(gy.at[0, ny1], gy.at[0, ny1], 4, y_peer(1)).wait_recv()
        for d in zs:
            remote(gy.at[0], gy.at[d], 6, z_peer(d)).start()

    passes_first = b >= n_branch // 2 - 1
    pl.when(passes_first)(pass_on)
    l_sk2.wait()
    sk2t[...] = jnp.concatenate([sk2[0].T, sk2[1].T], 1)
    l_near.wait()
    l_list1.wait()
    l_list2.wait()

    def rims(wait_k, take):
        for side, there, copies in ((0, has_lower, up), (1, has_upper, down)):
            pl.when(there)(lambda copies=copies: copies[wait_k].wait_recv())
            take(side, side * (RIM + leaves))

    def rim_features(side, base):
        source, _ = features(hc[side])
        flat = source.T.astype(BF16)
        for k in range(RIM):
            fs[base + k] = flat[k * LEAF : (k + 1) * LEAF]

    def rim_vectors(side, base):
        for i in range(RIM):
            high, low = split(hv[side, :, i * LEAF : (i + 1) * LEAF] * LN2)
            vw[base + i, :NV] = high
            vw[base + i, NV:] = low

    rims(0, rim_features)
    rims(1, rim_vectors)

    def near_leaves(first_leaf):
        items = [(first_leaf + u, pair) for u in range(BLOCK) for pair in PAIRS]

        def slots(i, pair):
            found = []
            for j in pair:
                named = near[j, i]
                slot = (named // (n_sub * leaves) - b) * leaves + named % leaves + RIM
                found.append(jnp.clip(slot, 0, leaves + 2 * RIM - 1))
            return found

        squares, tiles, acc = {}, {}, None
        for step in range(len(items) + 2):
            if step < len(items):
                i, pair = items[step]
                named = slots(i, pair)
                sources = jnp.concatenate([fs[m] for m in named], 0)
                squares[step] = named, dot_bf16(sources, ft[:, leaf_cols(i)])
            if 0 <= step - 1 < len(items):
                named, square = squares.pop(step - 1)
                tiles[step - 1] = named, jnp.concatenate(split(matern_of(square)), 1)
            if step >= 2:
                i, pair = items[step - 2]
                named, tile = tiles.pop(step - 2)
                part = dot_bf16(jnp.concatenate([vw[m] for m in named], 1), tile)
                acc = part if acc is None else acc + part
                if pair == PAIRS[-1]:
                    out[:, leaf_cols(i)] = fold(acc) + NUGGET * vec[:, leaf_cols(i)]
                    acc = None

    def place_of(branch):
        return (z + n_z - branch // n_y) % n_z, (y + n_y - branch % n_y) % n_y

    def far_tile(target, sources):
        column = (jnp.concatenate([target[:, :RANK], target[:, RANK : 2 * RANK]], 0) * SCALE).T
        sx = jnp.concatenate([row[:, :RANK] for row in sources], 1) * SCALE
        sy = jnp.concatenate([row[:, RANK : 2 * RANK] for row in sources], 1) * SCALE
        dx = sx - column[:, 0:1]
        dy = sy - column[:, 1:2]
        return matern_of(dx * dx + dy * dy) * LN2

    def group_field():
        remote(gs.at[ny1], gs.at[ny1], 7, y_peer(1)).wait_recv()
        remote(gz.at[0, nz1], gz.at[0, nz1], 5, z_peer(1)).wait_recv()
        for d in ys:
            remote(gz.at[0], gz.at[d], 9, y_peer(d)).start()
        sources, coeffs = [], []
        for k in range(8):
            m = list2[0, k]
            dz, dy = place_of(m)
            sources.append(sk2t[pl.ds(m, 1)])
            block = gs[dy, dz][0:rows]
            coeffs.append(jnp.concatenate([block[:, RANK * q : RANK * (q + 1)] for q in range(4)], 0))
        field = dot_f32(jnp.concatenate(coeffs, 1), far_tile(sk2t[pl.ds(b, 1)], sources), NT)
        fc[0] = jnp.concatenate([field[rows * q : rows * (q + 1)] for q in range(4)], 1)
        for d in ss:
            remote(fc.at[0], fc.at[d], 10, sub_peer(d)).start()

    blocks = leaves // BLOCK
    pass_step = jnp.where(passes_first, blocks, jnp.where(z >= n_z // 4, 1, 2))
    group_step = jnp.where(z >= n_z // 2, 2, jnp.where(z >= n_z // 4, 3, blocks))

    def near_block(t, c):
        pl.when(t == pass_step)(pass_on)
        pl.when(t == group_step)(group_field)
        near_leaves(t * BLOCK)
        return c

    lax.fori_loop(0, blocks, near_block, 0)
    pl.when(group_step == blocks)(group_field)

    remote(gy.at[nz1], gy.at[nz1], 6, z_peer(1)).wait_recv()
    remote(gz.at[ny1], gz.at[ny1], 9, y_peer(1)).wait_recv()
    sources, coeffs = [], []
    for k in range(8):
        dz, dy = place_of(list1[0, k] // n_sub)
        sources.append(gs[dy, dz][rows : rows + 1])
        block = jnp.concatenate([gy[dz, dy, 0], gy[dz, dy, 1], gy[dz, dy, 2], gz[dy, dz]], 0)
        coeffs += [block[:, :NV], block[:, NV:]]
    field = dot_f32(far_tile(gs[0, 0][rows : rows + 1], sources), jnp.concatenate(coeffs, 0))
    remote(fc.at[ns1], fc.at[ns1], 10, sub_peer(1)).wait_recv()
    packed = jnp.concatenate([fc[(s + n_sub - p) % n_sub] for p in range(n_sub)], 0)
    group_t = jnp.concatenate([packed[:, RANK * q : RANK * (q + 1)] for q in range(4)], 0)
    field = field + dot_f32(ntr[0], group_t, NT)
    fh, fl = split(field.T)
    lhs = jnp.concatenate([fh, fh, fl], 1)

    def far(i, c):
        cols = pl.ds(pl.multiple_of(i * 2 * LEAF, 2 * LEAF), 2 * LEAF)
        out[:, cols] += dot_bf16(lhs, w3[:, cols])
        return c

    lax.fori_loop(0, leaves // 2, far, 0, unroll=8)

    def finish(copies):
        for copy in copies:
            copy.wait_send()

    pl.when(has_lower)(lambda: finish(down))
    pl.when(has_upper)(lambda: finish(up))
    for ref, k in (
        (gy.at[0, ny1], 4), (gz.at[0, nz1], 5), (gy.at[nz1], 6), (gs.at[ny1], 7),
        (ru.at[ns1], 8), (gz.at[ny1], 9), (fc.at[ns1], 10), (gs.at[0, nz1], 11),
    ):
        remote(ref, ref, k, sub_peer(1)).wait_send()


def body(sizes, vectors, coords, basis, leaf_transfer, node_transfer, skel_one, skel_two, near_list, list_one, list_two):
    n_branch, n_sub, n_y = sizes
    n_z = n_branch // n_y
    leaves = leaf_transfer.shape[0]
    window = leaves + 2 * RIM
    rows = 16 // n_sub
    rim = RIM * LEAF
    operands = (
        vectors, coords, basis, leaf_transfer, node_transfer, skel_one,
        jnp.transpose(skel_two, (1, 2, 0)), near_list.T, list_one, list_two,
    )
    held = [pltpu.VMEM(a.shape, F32) for a in operands[:7]] + [pltpu.SMEM(a.shape, jnp.int32) for a in operands[7:]]
    return pl.pallas_call(
        functools.partial(kernel, sizes),
        out_shape=jax.ShapeDtypeStruct(vectors.shape, F32),
        in_specs=[pl.BlockSpec(memory_space=pltpu.HBM)] * 10,
        out_specs=pl.BlockSpec(memory_space=pltpu.VMEM),
        scratch_shapes=[
            *held,
            pltpu.VMEM((2, NV, rim), F32),
            pltpu.VMEM((2, 2, rim), F32),
            pltpu.VMEM((window, 2 * NV, LEAF), BF16),
            pltpu.VMEM((window, LEAF, FEATURES), BF16),
            pltpu.VMEM((FEATURES, leaves * LEAF), BF16),
            pltpu.VMEM((3 * RANK, leaves * LEAF), BF16),
            pltpu.VMEM((n_branch, 2 * RANK), F32),
            pltpu.VMEM((n_z, n_y, 3, 4, 128), F32),
            pltpu.VMEM((n_y, n_z, 4, 128), F32),
            pltpu.VMEM((n_y, n_z, 2 * rows, 128), F32),
            pltpu.VMEM((n_sub, rows, 128), F32),
            pltpu.VMEM((n_sub, rows, 128), F32),
            pltpu.VMEM((n_sub, rows, 128), F32),
            pltpu.SemaphoreType.DMA((10,)),
            pltpu.SemaphoreType.DMA((12,)),
            pltpu.SemaphoreType.DMA((12,)),
            pltpu.SemaphoreType.REGULAR,
        ],
        compiler_params=pltpu.CompilerParams(
            collective_id=0, has_side_effects=True, vmem_limit_bytes=VMEM_LIMIT
        ),
        name="h2_product",
    )(*operands)


def solution(mesh, y_count=Y_COUNT):
    both = ("branch", "sub")
    return jax.shard_map(
        functools.partial(body, (mesh.shape["branch"], mesh.shape["sub"], y_count)),
        mesh=mesh,
        in_specs=(
            P(None, both),
            P(None, both),
            P(None, both),
            P(both, None, None),
            P(both, None, None),
            P(both, None, None),
            P(),
            P(both, None),
            P(both, None),
            P("branch", None),
        ),
        out_specs=P(None, both),
        check_vma=False,
    )
```

```python
import functools
import math

import jax
import jax.numpy as jnp
from jax import lax
from jax.experimental import pallas as pl
from jax.experimental.pallas import tpu as pltpu
from jax.sharding import PartitionSpec as P

MESH = pl.DeviceIdType.MESH
F32 = jnp.float32
BF16 = jnp.bfloat16
NUGGET = 0.5
LOG2E = math.log2(math.e)
LN2 = math.log(2.0)
SCALE = math.sqrt(3.0) / 0.7 * LOG2E
Y_COUNT = 8
LEAF = 128
RANK = 32
NV = 64
RIM = 8
BLOCK = 8
PAIRS = ((0, 1), (2, 3), (4, 5), (6, 7), (8,))
EXACT = lax.Precision.HIGHEST
CENTRE = 1.5
VMEM_LIMIT = 62 * 2**20
FEATURES = 32
NN, NT, TN = ((1,), (0,)), ((1,), (1,)), ((0,), (0,))


def split(x):
    high = x.astype(BF16)
    return high, (x - high.astype(F32)).astype(BF16)


def split3(x):
    first = x.astype(BF16).astype(F32)
    rest = x - first
    second = rest.astype(BF16).astype(F32)
    return first, second, rest - second


def matern_of(square):
    square = jnp.maximum(square, 1e-30)
    dist = square * lax.rsqrt(square)
    return (dist + LOG2E) * jnp.exp2(-dist)


def features(coords):
    w = (coords - CENTRE) * SCALE
    norm = w[0:1] * w[0:1] + w[1:2] * w[1:2]
    s1, s2, s3 = split3(w)
    norms = split3(norm)
    ones = [jnp.ones_like(norm)] * 3
    zeros = jnp.zeros((FEATURES - 18, w.shape[1]), F32)
    t1, t2, t3 = -2.0 * s1, -2.0 * s2, -2.0 * s3
    source = jnp.concatenate([s1, s1, s2, s2, s1, s3, *norms, *ones, zeros], 0)
    target = jnp.concatenate([t1, t2, t1, t2, t3, t1, *ones, *norms, zeros], 0)
    return source, target


def dot_f32(a, b, dims=NN):
    return lax.dot_general(a, b, (dims, ((), ())), precision=EXACT, preferred_element_type=F32)


def dot_high(a, b, dims=NN):
    return lax.dot_general(a, b, (dims, ((), ())), precision=lax.Precision.HIGH, preferred_element_type=F32)


def dot_bf16(a, b, dims=NN):
    return lax.dot_general(a, b, (dims, ((), ())), preferred_element_type=F32)


def fold(r):
    half = r.shape[0] // 2, r.shape[1] // 2
    return r[: half[0], : half[1]] + r[half[0] :, : half[1]] + r[: half[0], half[1] :] + r[half[0] :, half[1] :]


def leaf_cols(i):
    return pl.ds(pl.multiple_of(i * LEAF, LEAF), LEAF)


def kernel(sizes, *refs):
    operands, out = refs[:10], refs[10]
    vec, crd, bas, ltr, ntr, sk1, sk2, near, list1, list2 = refs[11:21]
    hv, hc, vw, fs, ft, w3, sk2t, info, early, column, mix, part, parts, own_field, fc, load, send, recv, later = refs[21:]
    n_branch, n_sub, n_y = sizes
    n_z = n_branch // n_y
    leaves = ltr.shape[0]
    ny1, nz1, ns1 = pl.ds(1, n_y - 1), pl.ds(1, n_z - 1), pl.ds(1, n_sub - 1)
    b = lax.axis_index("branch")
    s = lax.axis_index("sub")
    z = b // n_y
    y = b % n_y

    loads = [pltpu.make_async_copy(operands[k], refs[11 + k], load.at[k]) for k in range(10)]
    l_vec, l_crd, l_bas, l_ltr, l_ntr, l_sk1, l_sk2, l_near, l_list1, l_list2 = loads
    for copy in (l_ltr, l_bas, l_vec, l_crd, l_ntr, l_sk1, l_sk2, l_near, l_list1, l_list2):
        copy.start()

    def y_peer(d):
        return z * n_y + (y + d) % n_y, s

    def z_peer(d):
        return ((z + d) % n_z) * n_y + y, s

    def sub_peer(d):
        return b, (s + d) % n_sub

    def remote(src, dst, k, peer):
        return pltpu.make_async_remote_copy(
            src_ref=src, dst_ref=dst, send_sem=send.at[k], recv_sem=recv.at[k], device_id=peer, device_id_type=MESH
        )

    def signal(sem, peer):
        pl.semaphore_signal(sem, inc=1, device_id=peer, device_id_type=MESH)

    ys, zs, ss = range(1, n_y), range(1, n_z), range(1, n_sub)
    has_lower, has_upper = b > 0, b < n_branch - 1
    lower, upper = (b - 1, s), (b + 1, s)

    barrier = pltpu.get_barrier_semaphore()
    pl.when(has_lower)(lambda: signal(barrier, lower))
    pl.when(has_upper)(lambda: signal(barrier, upper))
    for d in ss:
        signal(barrier, sub_peer(d))
    for d in ys:
        signal(barrier, y_peer(d))
    for other in range(1, n_z):
        pl.when(other > z)(lambda other=other: signal(barrier, (other * n_y + y, s)))

    starts_late = z >= n_z // 2
    met = n_sub - 1 + n_y - 1 + z + has_lower.astype(jnp.int32) + has_upper.astype(jnp.int32)

    def along_z(ref, k, higher):
        for d in zs:
            pl.when(z + d < n_z if higher else z + d >= n_z)(
                lambda d=d: remote(ref.at[0], ref.at[d], k, z_peer(d)).start()
            )

    def enter():
        pl.semaphore_wait(barrier, met)
        for other in range(n_z - 1):
            pl.when(other < z)(lambda other=other: signal(later, (other * n_y + y, s)))
        l_sk1.wait()
        l_list1.wait()
        l_list2.wait()
        l_ntr.wait()
        row = [sk1[0, 0:1], sk1[0, 1:2], list1[...].astype(F32), list2[...].astype(F32)]
        row = jnp.concatenate(row + [jnp.zeros((1, 128 - 2 * RANK - 16), F32)], 1)
        info[0] = row
        early[0, 8:9] = row
        early[0, 0:8] = jnp.concatenate([ntr[0, 8 * k : 8 * (k + 1)] for k in range(4)], 1)
        for d in ys:
            remote(info.at[0], info.at[d], 4, y_peer(d)).start()
        along_z(early, 8, False)

    pl.when(starts_late)(enter)

    for side, missing in ((0, b == 0), (1, b == n_branch - 1)):

        @pl.when(missing)
        def _(side=side):
            hv[side] = jnp.zeros(hv.shape[1:], F32)
            hc[side] = jnp.zeros(hc.shape[1:], F32)

    l_ltr.wait()
    l_bas.wait()

    def make_w(i, c):
        cols = leaf_cols(i)
        bh, bl = split(bas[:, cols])
        lh, ll = split(ltr[i])
        w = dot_bf16(jnp.concatenate([lh, lh, ll], 0), jnp.concatenate([bh, bl, bh], 0), TN)
        wh, wl = split(w)
        w3[:RANK, cols] = wh
        w3[RANK : 2 * RANK, cols] = wl
        w3[2 * RANK :, cols] = wh
        return c

    lax.fori_loop(0, leaves, make_w, 0, unroll=16)

    l_vec.wait()

    def own_vectors(i, c):
        high, low = split(vec[:, leaf_cols(i)] * LN2)
        vw[RIM + i, :NV] = high
        vw[RIM + i, NV:] = low
        return c

    lax.fori_loop(0, leaves, own_vectors, 0, unroll=8)
    own = jnp.concatenate([vw[RIM + i] for i in range(leaves)], 1)
    coeff_t = fold(dot_bf16(own, w3[: 2 * RANK], NT)) * (1.0 / LN2)
    coeff = coeff_t.T
    column[0] = jnp.concatenate([coeff[: RANK // 2], coeff[RANK // 2 :]], 1)
    pl.when(jnp.logical_not(starts_late))(enter)
    along_z(column, 5, False)

    rim = RIM * LEAF
    first, last = pl.ds(0, rim), pl.ds(leaves * LEAF - rim, rim)
    top, bottom = pl.ds(0, NV // 2), pl.ds(NV // 2, NV // 2)
    down = [
        remote(crd.at[:, first], hc.at[1], 0, lower),
        remote(vec.at[top, first], hv.at[1, top], 2, lower),
        remote(vec.at[bottom, first], hv.at[1, bottom], 9, lower),
    ]
    up = [
        remote(crd.at[:, last], hc.at[0], 1, upper),
        remote(vec.at[top, last], hv.at[0, top], 3, upper),
        remote(vec.at[bottom, last], hv.at[0, bottom], 10, upper),
    ]

    def start_all(copies):
        for copy in copies:
            copy.start()

    lower_early = has_lower & jnp.logical_not(starts_late & (y == 0))
    upper_early = has_upper & jnp.logical_not(starts_late & (y == n_y - 1))
    lower_late = has_lower & starts_late & (y == 0)
    upper_late = has_upper & starts_late & (y == n_y - 1)

    l_crd.wait()
    pl.when(lower_early)(lambda: start_all(down))
    pl.when(upper_early)(lambda: start_all(up))
    wide = 8 * LEAF

    def own_features(i, c):
        cols = pl.ds(pl.multiple_of(i * wide, wide), wide)
        source, target = features(crd[:, cols])
        ft[:, cols] = target.astype(BF16)
        flat = source.T.astype(BF16)
        for k in range(8):
            fs[RIM + i * 8 + k] = flat[k * LEAF : (k + 1) * LEAF]
        return c

    lax.fori_loop(0, leaves // 8, own_features, 0)
    @pl.when(z < n_z - 1)
    def _():
        pl.semaphore_wait(later, n_z - 1 - z)

    along_z(early, 8, True)
    along_z(column, 5, True)
    pl.when(lower_late)(lambda: start_all(down[:2]))
    pl.when(upper_late)(lambda: start_all(up[:2]))
    l_sk2.wait()
    sk2t[...] = jnp.concatenate([sk2[0].T, sk2[1].T], 1)

    def prepare_parts():
        remote(info.at[ny1], info.at[ny1], 4, y_peer(1)).wait_recv()
        remote(early.at[nz1], early.at[nz1], 8, z_peer(1)).wait_recv()
        pl.when(lower_late)(lambda: start_all(down[2:]))
        pl.when(upper_late)(lambda: start_all(up[2:]))
        target = jnp.concatenate([info[(n_y - d) % n_y] for d in range(n_y)], 0)
        group = [sk2t[pl.ds(z * n_y + (y + d) % n_y, 1)] for d in range(n_y)]
        line = [jnp.concatenate([target[d : d + 1, RANK * k : RANK * (k + 1)] for d in range(n_y)], 1) for k in range(2)]
        line += [jnp.concatenate([g[:, RANK * k : RANK * (k + 1)] for g in group], 1) for k in range(2)]
        at = (jnp.concatenate(line + [jnp.zeros((4, n_y * RANK), F32)], 0) * SCALE).T
        node_rows = [early[d, 8:9] for d in range(n_z)]
        group_rows = [sk2t[pl.ds((z + n_z - d) % n_z * n_y + y, 1)] for d in range(n_z)]
        for level, (source, scale) in enumerate(((node_rows, n_sub), (group_rows, 1))):
            sx = jnp.concatenate([r[:, :RANK] for r in source], 1) * SCALE
            sy = jnp.concatenate([r[:, RANK : 2 * RANK] for r in source], 1) * SCALE
            dx = at[:, 2 * level : 2 * level + 1] - sx
            dy = at[:, 2 * level + 1 : 2 * level + 2] - sy
            names = []
            for d in range(n_z):
                name = ((z + n_z - d) % n_z * n_y + y) * scale + (s if scale > 1 else 0)
                names.append(jnp.full((1, RANK), name.astype(F32), F32))
            names = jnp.concatenate(names, 1)
            count = jnp.zeros((n_y, n_z * RANK), F32)
            for k in range(8):
                lane = 2 * RANK + 8 * level + k
                count = count + (target[:, lane : lane + 1] == names).astype(F32)
            count = jnp.concatenate([jnp.broadcast_to(count[d : d + 1], (RANK, n_z * RANK)) for d in range(n_y)], 0)
            tile = matern_of(dx * dx + dy * dy) * (count * LN2)
            if level == 1:
                moved = []
                for d in range(n_z):
                    transfer = jnp.concatenate([early[d, 0:8, RANK * k : RANK * (k + 1)] for k in range(4)], 0)
                    moved.append(dot_high(tile[:, d * RANK : (d + 1) * RANK], transfer, NT))
                tile = jnp.concatenate(moved, 1)
            high, low = split(tile)
            mix[level * n_y * RANK : (level + 1) * n_y * RANK] = jnp.concatenate([high, high, low], 1)

    def send_parts():
        remote(column.at[nz1], column.at[nz1], 5, z_peer(1)).wait_recv()
        coeffs = []
        for d in range(n_z):
            coeffs += [column[d, :, :NV], column[d, :, NV:]]
        high, low = split(jnp.concatenate(coeffs, 0))
        fields = dot_bf16(mix[...], jnp.concatenate([high, low, high], 0))
        for d in range(n_y):
            at = d * RANK
            part[d] = jnp.concatenate([fields[at : at + RANK], fields[n_y * RANK + at : n_y * RANK + at + RANK]], 1)
        for d in ys:
            remote(part.at[d], parts.at[d], 6, y_peer(d)).start()

    def both_parts():
        prepare_parts()
        send_parts()

    parts_first = z >= n_z // 2 - 1
    pl.when(parts_first)(both_parts)
    l_near.wait()

    def arrived(copies):
        for copy in copies:
            copy.wait_recv()

    def rims(waits, take):
        for side, there, copies in ((0, has_lower, up), (1, has_upper, down)):
            pl.when(there)(lambda copies=copies: arrived(copies[waits]))
            take(side, side * (RIM + leaves))

    def rim_features(side, base):
        source, _ = features(hc[side])
        flat = source.T.astype(BF16)
        for k in range(RIM):
            fs[base + k] = flat[k * LEAF : (k + 1) * LEAF]

    def rim_vectors(side, base):
        for i in range(RIM):
            high, low = split(hv[side, :, i * LEAF : (i + 1) * LEAF] * LN2)
            vw[base + i, :NV] = high
            vw[base + i, NV:] = low

    rims(slice(0, 1), rim_features)
    rims(slice(1, 3), rim_vectors)

    def near_leaves(first_leaf):
        items = [(first_leaf + u, pair) for u in range(BLOCK) for pair in PAIRS]

        def slots(i, pair):
            found = []
            for j in pair:
                named = near[j, i]
                slot = (named // (n_sub * leaves) - b) * leaves + named % leaves + RIM
                found.append(jnp.clip(slot, 0, leaves + 2 * RIM - 1))
            return found

        squares, tiles, acc = {}, {}, None
        for step in range(len(items) + 2):
            if step < len(items):
                i, pair = items[step]
                named = slots(i, pair)
                sources = jnp.concatenate([fs[m] for m in named], 0)
                squares[step] = named, dot_bf16(sources, ft[:, leaf_cols(i)])
            if 0 <= step - 1 < len(items):
                named, square = squares.pop(step - 1)
                tiles[step - 1] = named, jnp.concatenate(split(matern_of(square)), 1)
            if step >= 2:
                i, pair = items[step - 2]
                named, tile = tiles.pop(step - 2)
                part = dot_bf16(jnp.concatenate([vw[m] for m in named], 1), tile)
                acc = part if acc is None else acc + part
                if pair == PAIRS[-1]:
                    out[:, leaf_cols(i)] = fold(acc) + NUGGET * vec[:, leaf_cols(i)]
                    acc = None

    def send_group():
        remote(parts.at[ny1], parts.at[ny1], 6, y_peer(1)).wait_recv()
        field = part[0]
        for d in ys:
            field = field + parts[d]
        own_field[...] = field
        fc[0] = jnp.concatenate([field[: RANK // 2, NV:], field[RANK // 2 :, NV:]], 1)
        for d in ss:
            remote(fc.at[0], fc.at[d], 7, sub_peer(d)).start()

    parts_step = jnp.where(parts_first, leaves // BLOCK, 1)
    group_step = jnp.where(parts_first, 2, 3)

    def near_block(t, c):
        pl.when(t == parts_step)(both_parts)
        pl.when(t == group_step)(send_group)
        near_leaves(t * BLOCK)
        return c

    lax.fori_loop(0, leaves // BLOCK, near_block, 0)

    remote(fc.at[ns1], fc.at[ns1], 7, sub_peer(1)).wait_recv()
    group = fc[0]
    for d in ss:
        group = group + fc[d]
    group = jnp.concatenate([group[:, :NV], group[:, NV:]], 0)
    field = own_field[:, :NV] + dot_f32(ntr[0], group)
    fh, fl = split(field.T)
    lhs = jnp.concatenate([fh, fh, fl], 1)

    def far(i, c):
        cols = pl.ds(pl.multiple_of(i * 2 * LEAF, 2 * LEAF), 2 * LEAF)
        out[:, cols] += dot_bf16(lhs, w3[:, cols])
        return c

    lax.fori_loop(0, leaves // 2, far, 0, unroll=8)

    def finish(copies):
        for copy in copies:
            copy.wait_send()

    pl.when(has_lower)(lambda: finish(down))
    pl.when(has_upper)(lambda: finish(up))
    for ref, k in ((info.at[ny1], 4), (column.at[nz1], 5), (parts.at[ny1], 6), (fc.at[ns1], 7), (early.at[nz1], 8)):
        remote(ref, ref, k, sub_peer(1)).wait_send()


def body(sizes, vectors, coords, basis, leaf_transfer, node_transfer, skel_one, skel_two, near_list, list_one, list_two):
    n_branch, n_sub, n_y = sizes
    n_z = n_branch // n_y
    leaves = leaf_transfer.shape[0]
    window = leaves + 2 * RIM
    rim = RIM * LEAF
    operands = (
        vectors, coords, basis, leaf_transfer, node_transfer, skel_one,
        jnp.transpose(skel_two, (1, 2, 0)), near_list.T, list_one, list_two,
    )
    held = [pltpu.VMEM(a.shape, F32) for a in operands[:7]] + [pltpu.SMEM(operands[7].shape, jnp.int32)]
    held += [pltpu.VMEM(a.shape, jnp.int32) for a in operands[8:]]
    return pl.pallas_call(
        functools.partial(kernel, sizes),
        out_shape=jax.ShapeDtypeStruct(vectors.shape, F32),
        in_specs=[pl.BlockSpec(memory_space=pltpu.HBM)] * 10,
        out_specs=pl.BlockSpec(memory_space=pltpu.VMEM),
        scratch_shapes=[
            *held,
            pltpu.VMEM((2, NV, rim), F32),
            pltpu.VMEM((2, 2, rim), F32),
            pltpu.VMEM((window, 2 * NV, LEAF), BF16),
            pltpu.VMEM((window, LEAF, FEATURES), BF16),
            pltpu.VMEM((FEATURES, leaves * LEAF), BF16),
            pltpu.VMEM((3 * RANK, leaves * LEAF), BF16),
            pltpu.VMEM((n_branch, 2 * RANK), F32),
            pltpu.VMEM((n_y, 1, 128), F32),
            pltpu.VMEM((n_z, 9, 128), F32),
            pltpu.VMEM((n_z, RANK // 2, 128), F32),
            pltpu.VMEM((2 * n_y * RANK, 3 * n_z * RANK), BF16),
            pltpu.VMEM((n_y, RANK, 128), F32),
            pltpu.VMEM((n_y, RANK, 128), F32),
            pltpu.VMEM((RANK, 128), F32),
            pltpu.VMEM((n_sub, RANK // 2, 128), F32),
            pltpu.SemaphoreType.DMA((10,)),
            pltpu.SemaphoreType.DMA((11,)),
            pltpu.SemaphoreType.DMA((11,)),
            pltpu.SemaphoreType.REGULAR,
        ],
        compiler_params=pltpu.CompilerParams(
            collective_id=0, has_side_effects=True, vmem_limit_bytes=VMEM_LIMIT
        ),
        name="h2_product",
    )(*operands)


def solution(mesh, y_count=Y_COUNT):
    both = ("branch", "sub")
    return jax.shard_map(
        functools.partial(body, (mesh.shape["branch"], mesh.shape["sub"], y_count)),
        mesh=mesh,
        in_specs=(
            P(None, both),
            P(None, both),
            P(None, both),
            P(both, None, None),
            P(both, None, None),
            P(both, None, None),
            P(),
            P(both, None),
            P(both, None),
            P("branch", None),
        ),
        out_specs=P(None, both),
        check_vma=False,
    )
```

```python
import functools
import math

import jax
import jax.numpy as jnp
from jax import lax
from jax.experimental import pallas as pl
from jax.experimental.pallas import tpu as pltpu
from jax.sharding import PartitionSpec as P

MESH = pl.DeviceIdType.MESH
F32 = jnp.float32
BF16 = jnp.bfloat16
NUGGET = 0.5
LOG2E = math.log2(math.e)
LN2 = math.log(2.0)
SCALE = math.sqrt(3.0) / 0.7 * LOG2E
Y_COUNT = 8
LEAF = 128
RANK = 32
NV = 64
RIM = 8
BLOCK = 8
PAIRS = ((0, 1), (2, 3), (4, 5), (6, 7), (8,))
EXACT = lax.Precision.HIGHEST
CENTRE = 1.5
VMEM_LIMIT = 62 * 2**20
FEATURES = 32
CHUNKS = 4
NN, NT, TN = ((1,), (0,)), ((1,), (1,)), ((0,), (0,))


def split(x):
    high = x.astype(BF16)
    return high, (x - high.astype(F32)).astype(BF16)


def split3(x):
    first = x.astype(BF16).astype(F32)
    rest = x - first
    second = rest.astype(BF16).astype(F32)
    return first, second, rest - second


def matern_of(square):
    square = jnp.maximum(square, 1e-30)
    dist = square * lax.rsqrt(square)
    return (dist + LOG2E) * jnp.exp2(-dist)


def features(coords):
    w = (coords - CENTRE) * SCALE
    norm = w[0:1] * w[0:1] + w[1:2] * w[1:2]
    s1, s2, s3 = split3(w)
    norms = split3(norm)
    ones = [jnp.ones_like(norm)] * 3
    zeros = jnp.zeros((FEATURES - 18, w.shape[1]), F32)
    t1, t2, t3 = -2.0 * s1, -2.0 * s2, -2.0 * s3
    source = jnp.concatenate([s1, s1, s2, s2, s1, s3, *norms, *ones, zeros], 0)
    target = jnp.concatenate([t1, t2, t1, t2, t3, t1, *ones, *norms, zeros], 0)
    return source, target


def dot_f32(a, b, dims=NN):
    return lax.dot_general(a, b, (dims, ((), ())), precision=EXACT, preferred_element_type=F32)


def dot_high(a, b, dims=NN):
    return lax.dot_general(a, b, (dims, ((), ())), precision=lax.Precision.HIGH, preferred_element_type=F32)


def dot_bf16(a, b, dims=NN):
    return lax.dot_general(a, b, (dims, ((), ())), preferred_element_type=F32)


def fold(r):
    half = r.shape[0] // 2, r.shape[1] // 2
    return r[: half[0], : half[1]] + r[half[0] :, : half[1]] + r[: half[0], half[1] :] + r[half[0] :, half[1] :]


def leaf_cols(i):
    return pl.ds(pl.multiple_of(i * LEAF, LEAF), LEAF)


def kernel(sizes, *refs):
    operands, result = refs[:10], refs[10]
    vec, crd, bas, ltr, ntr, sk1, sk2, near, list1, list2 = refs[11:21]
    out, hv, hc, vw, fs, ft, w3, sk2t, info, early, column, mix, part, parts, own_field, fc, load, store, send, recv, later = refs[21:]
    n_branch, n_sub, n_y = sizes
    n_z = n_branch // n_y
    leaves = ltr.shape[0]
    ny1, nz1, ns1 = pl.ds(1, n_y - 1), pl.ds(1, n_z - 1), pl.ds(1, n_sub - 1)
    b = lax.axis_index("branch")
    s = lax.axis_index("sub")
    z = b // n_y
    y = b % n_y

    loads = [pltpu.make_async_copy(operands[k], refs[11 + k], load.at[k]) for k in range(10)]
    l_vec, l_crd, l_bas, l_ltr, l_ntr, l_sk1, l_sk2, l_near, l_list1, l_list2 = loads
    for copy in (l_ltr, l_bas, l_vec, l_crd, l_ntr, l_sk1, l_sk2, l_near, l_list1, l_list2):
        copy.start()

    def y_peer(d):
        return z * n_y + (y + d) % n_y, s

    def z_peer(d):
        return ((z + d) % n_z) * n_y + y, s

    def sub_peer(d):
        return b, (s + d) % n_sub

    def remote(src, dst, k, peer):
        return pltpu.make_async_remote_copy(
            src_ref=src, dst_ref=dst, send_sem=send.at[k], recv_sem=recv.at[k], device_id=peer, device_id_type=MESH
        )

    def signal(sem, peer):
        pl.semaphore_signal(sem, inc=1, device_id=peer, device_id_type=MESH)

    ys, zs, ss = (sorted(range(1, n), key=lambda d: (-min(d, n - d), d)) for n in (n_y, n_z, n_sub))
    has_lower, has_upper = b > 0, b < n_branch - 1
    lower, upper = (b - 1, s), (b + 1, s)

    barrier = pltpu.get_barrier_semaphore()
    pl.when(has_lower)(lambda: signal(barrier, lower))
    pl.when(has_upper)(lambda: signal(barrier, upper))
    for d in ss:
        signal(barrier, sub_peer(d))
    for d in ys:
        signal(barrier, y_peer(d))
    for other in range(1, n_z):
        pl.when(other > z)(lambda other=other: signal(barrier, (other * n_y + y, s)))

    starts_late = z >= n_z // 2
    met = n_sub - 1 + n_y - 1 + z + has_lower.astype(jnp.int32) + has_upper.astype(jnp.int32)

    def along_z(ref, k, higher):
        for d in zs:
            pl.when(z + d < n_z if higher else z + d >= n_z)(
                lambda d=d: remote(ref.at[0], ref.at[d], k, z_peer(d)).start()
            )

    def enter():
        pl.semaphore_wait(barrier, met)
        for other in range(n_z - 1):
            pl.when(other < z)(lambda other=other: signal(later, (other * n_y + y, s)))
        l_sk1.wait()
        l_list1.wait()
        l_list2.wait()
        l_ntr.wait()
        row = [sk1[0, 0:1], sk1[0, 1:2], list1[...].astype(F32), list2[...].astype(F32)]
        row = jnp.concatenate(row + [jnp.zeros((1, 128 - 2 * RANK - 16), F32)], 1)
        info[0] = row
        early[0, 8:9] = row
        early[0, 0:8] = jnp.concatenate([ntr[0, 8 * k : 8 * (k + 1)] for k in range(4)], 1)
        for d in ys:
            remote(info.at[0], info.at[d], 4, y_peer(d)).start()
        along_z(early, 8, False)

    for side, missing in ((0, b == 0), (1, b == n_branch - 1)):

        @pl.when(missing)
        def _(side=side):
            hv[side] = jnp.zeros(hv.shape[1:], F32)
            hc[side] = jnp.zeros(hc.shape[1:], F32)

    l_ltr.wait()
    l_bas.wait()

    def make_w(i, c):
        cols = leaf_cols(i)
        bh, bl = split(bas[:, cols])
        lh, ll = split(ltr[i])
        w = dot_bf16(jnp.concatenate([lh, lh, ll], 0), jnp.concatenate([bh, bl, bh], 0), TN)
        wh, wl = split(w)
        w3[:RANK, cols] = wh
        w3[RANK : 2 * RANK, cols] = wl
        w3[2 * RANK :, cols] = wh
        return c

    lax.fori_loop(0, leaves, make_w, 0, unroll=16)

    l_vec.wait()

    def own_vectors(i, c):
        high, low = split(vec[:, leaf_cols(i)] * LN2)
        vw[RIM + i, :NV] = high
        vw[RIM + i, NV:] = low
        return c

    lax.fori_loop(0, leaves, own_vectors, 0, unroll=8)
    pl.when(starts_late)(enter)
    own = jnp.concatenate([vw[RIM + i] for i in range(leaves)], 1)
    coeff_t = fold(dot_bf16(own, w3[: 2 * RANK], NT)) * (1.0 / LN2)
    coeff = coeff_t.T
    column[0] = jnp.concatenate([coeff[: RANK // 2], coeff[RANK // 2 :]], 1)
    pl.when(jnp.logical_not(starts_late))(enter)
    along_z(column, 5, False)

    rim = RIM * LEAF
    first, last = pl.ds(0, rim), pl.ds(leaves * LEAF - rim, rim)
    top, bottom = pl.ds(0, NV // 2), pl.ds(NV // 2, NV // 2)
    down = [
        remote(crd.at[:, first], hc.at[1], 0, lower),
        remote(vec.at[top, first], hv.at[1, top], 2, lower),
        remote(vec.at[bottom, first], hv.at[1, bottom], 9, lower),
    ]
    up = [
        remote(crd.at[:, last], hc.at[0], 1, upper),
        remote(vec.at[top, last], hv.at[0, top], 3, upper),
        remote(vec.at[bottom, last], hv.at[0, bottom], 10, upper),
    ]

    def start_all(copies):
        for copy in copies:
            copy.start()

    lower_early = has_lower & jnp.logical_not(starts_late & (y == 0))
    upper_early = has_upper & jnp.logical_not(starts_late & (y == n_y - 1))
    lower_late = has_lower & starts_late & (y == 0)
    upper_late = has_upper & starts_late & (y == n_y - 1)

    l_crd.wait()
    pl.when(lower_early)(lambda: start_all(down))
    pl.when(upper_early)(lambda: start_all(up))
    wide = 8 * LEAF

    def own_features(i, c):
        cols = pl.ds(pl.multiple_of(i * wide, wide), wide)
        source, target = features(crd[:, cols])
        ft[:, cols] = target.astype(BF16)
        flat = source.T.astype(BF16)
        for k in range(8):
            fs[RIM + i * 8 + k] = flat[k * LEAF : (k + 1) * LEAF]
        return c

    lax.fori_loop(0, leaves // 8, own_features, 0)
    @pl.when(z < n_z - 1)
    def _():
        pl.semaphore_wait(later, n_z - 1 - z)

    along_z(early, 8, True)
    along_z(column, 5, True)
    pl.when(lower_late)(lambda: start_all(down[:2]))
    l_sk2.wait()
    sk2t[...] = jnp.concatenate([sk2[0].T, sk2[1].T], 1)

    def prepare_parts():
        remote(info.at[ny1], info.at[ny1], 4, y_peer(1)).wait_recv()
        pl.when(lower_late)(lambda: start_all(down[2:]))
        pl.when(upper_late)(lambda: start_all(up[:2]))
        remote(early.at[nz1], early.at[nz1], 8, z_peer(1)).wait_recv()
        pl.when(upper_late)(lambda: start_all(up[2:]))
        target = jnp.concatenate([info[(n_y - d) % n_y] for d in range(n_y)], 0)
        group = [sk2t[pl.ds(z * n_y + (y + d) % n_y, 1)] for d in range(n_y)]
        line = [jnp.concatenate([target[d : d + 1, RANK * k : RANK * (k + 1)] for d in range(n_y)], 1) for k in range(2)]
        line += [jnp.concatenate([g[:, RANK * k : RANK * (k + 1)] for g in group], 1) for k in range(2)]
        at = (jnp.concatenate(line + [jnp.zeros((4, n_y * RANK), F32)], 0) * SCALE).T
        node_rows = [early[d, 8:9] for d in range(n_z)]
        group_rows = [sk2t[pl.ds((z + n_z - d) % n_z * n_y + y, 1)] for d in range(n_z)]
        for level, (source, scale) in enumerate(((node_rows, n_sub), (group_rows, 1))):
            sx = jnp.concatenate([r[:, :RANK] for r in source], 1) * SCALE
            sy = jnp.concatenate([r[:, RANK : 2 * RANK] for r in source], 1) * SCALE
            dx = at[:, 2 * level : 2 * level + 1] - sx
            dy = at[:, 2 * level + 1 : 2 * level + 2] - sy
            names = []
            for d in range(n_z):
                name = ((z + n_z - d) % n_z * n_y + y) * scale + (s if scale > 1 else 0)
                names.append(jnp.full((1, RANK), name.astype(F32), F32))
            names = jnp.concatenate(names, 1)
            count = jnp.zeros((n_y, n_z * RANK), F32)
            for k in range(8):
                lane = 2 * RANK + 8 * level + k
                count = count + (target[:, lane : lane + 1] == names).astype(F32)
            count = jnp.concatenate([jnp.broadcast_to(count[d : d + 1], (RANK, n_z * RANK)) for d in range(n_y)], 0)
            tile = matern_of(dx * dx + dy * dy) * (count * LN2)
            if level == 1:
                moved = []
                for d in range(n_z):
                    transfer = jnp.concatenate([early[d, 0:8, RANK * k : RANK * (k + 1)] for k in range(4)], 0)
                    moved.append(dot_high(tile[:, d * RANK : (d + 1) * RANK], transfer, NT))
                tile = jnp.concatenate(moved, 1)
            high, low = split(tile)
            mix[level * n_y * RANK : (level + 1) * n_y * RANK] = jnp.concatenate([high, high, low], 1)

    def send_parts():
        remote(column.at[nz1], column.at[nz1], 5, z_peer(1)).wait_recv()
        coeffs = []
        for d in range(n_z):
            coeffs += [column[d, :, :NV], column[d, :, NV:]]
        high, low = split(jnp.concatenate(coeffs, 0))
        fields = dot_bf16(mix[...], jnp.concatenate([high, low, high], 0))
        for d in range(n_y):
            at = d * RANK
            part[d] = jnp.concatenate([fields[at : at + RANK], fields[n_y * RANK + at : n_y * RANK + at + RANK]], 1)
        for d in ys:
            remote(part.at[d], parts.at[d], 6, y_peer(d)).start()

    def both_parts():
        prepare_parts()
        send_parts()

    parts_first = z >= n_z // 2 - 1
    pl.when(parts_first)(both_parts)
    l_near.wait()

    def arrived(copies):
        for copy in copies:
            copy.wait_recv()

    def rims(waits, take):
        for side, there, copies in ((0, has_lower, up), (1, has_upper, down)):
            pl.when(there)(lambda copies=copies: arrived(copies[waits]))
            take(side, side * (RIM + leaves))

    def rim_features(side, base):
        source, _ = features(hc[side])
        flat = source.T.astype(BF16)
        for k in range(RIM):
            fs[base + k] = flat[k * LEAF : (k + 1) * LEAF]

    def rim_vectors(side, base):
        for i in range(RIM):
            high, low = split(hv[side, :, i * LEAF : (i + 1) * LEAF] * LN2)
            vw[base + i, :NV] = high
            vw[base + i, NV:] = low

    rims(slice(0, 1), rim_features)
    rims(slice(1, 3), rim_vectors)

    def near_leaves(first_leaf):
        items = [(first_leaf + u, pair) for u in range(BLOCK) for pair in PAIRS]

        def slots(i, pair):
            found = []
            for j in pair:
                named = near[j, i]
                slot = (named // (n_sub * leaves) - b) * leaves + named % leaves + RIM
                found.append(jnp.clip(slot, 0, leaves + 2 * RIM - 1))
            return found

        squares, tiles, acc = {}, {}, None
        for step in range(len(items) + 2):
            if step < len(items):
                i, pair = items[step]
                named = slots(i, pair)
                sources = jnp.concatenate([fs[m] for m in named], 0)
                squares[step] = named, dot_bf16(sources, ft[:, leaf_cols(i)])
            if 0 <= step - 1 < len(items):
                named, square = squares.pop(step - 1)
                tiles[step - 1] = named, jnp.concatenate(split(matern_of(square)), 1)
            if step >= 2:
                i, pair = items[step - 2]
                named, tile = tiles.pop(step - 2)
                part = dot_bf16(jnp.concatenate([vw[m] for m in named], 1), tile)
                acc = part if acc is None else acc + part
                if pair == PAIRS[-1]:
                    out[:, leaf_cols(i)] = fold(acc) + NUGGET * vec[:, leaf_cols(i)]
                    acc = None

    def send_group():
        remote(parts.at[ny1], parts.at[ny1], 6, y_peer(1)).wait_recv()
        field = part[0]
        for d in ys:
            field = field + parts[d]
        own_field[...] = field
        fc[0] = jnp.concatenate([field[: RANK // 2, NV:], field[RANK // 2 :, NV:]], 1)
        for d in ss:
            remote(fc.at[0], fc.at[d], 7, sub_peer(d)).start()

    parts_step = jnp.where(parts_first, leaves // BLOCK, 1)
    group_step = jnp.where(parts_first, 2, 3)

    def near_block(t, c):
        pl.when(t == parts_step)(both_parts)
        pl.when(t == group_step)(send_group)
        near_leaves(t * BLOCK)
        return c

    lax.fori_loop(0, leaves // BLOCK, near_block, 0)

    remote(fc.at[ns1], fc.at[ns1], 7, sub_peer(1)).wait_recv()
    group = fc[0]
    for d in ss:
        group = group + fc[d]
    group = jnp.concatenate([group[:, :NV], group[:, NV:]], 0)
    field = own_field[:, :NV] + dot_f32(ntr[0], group)
    fh, fl = split(field.T)
    lhs = jnp.concatenate([fh, fh, fl], 1)

    wide = leaves * LEAF // CHUNKS
    stores = []
    for chunk in range(CHUNKS):
        for i in range(wide // (2 * LEAF)):
            cols = pl.ds(chunk * wide + i * 2 * LEAF, 2 * LEAF)
            out[:, cols] += dot_bf16(lhs, w3[:, cols])
        cols = pl.ds(chunk * wide, wide)
        stores.append(pltpu.make_async_copy(out.at[:, cols], result.at[:, cols], store.at[chunk]))
        stores[-1].start()

    def finish(copies):
        for copy in copies:
            copy.wait_send()

    pl.when(has_lower)(lambda: finish(down))
    pl.when(has_upper)(lambda: finish(up))
    for ref, k in ((info.at[ny1], 4), (column.at[nz1], 5), (parts.at[ny1], 6), (fc.at[ns1], 7), (early.at[nz1], 8)):
        remote(ref, ref, k, sub_peer(1)).wait_send()
    for copy in stores:
        copy.wait()


def body(sizes, vectors, coords, basis, leaf_transfer, node_transfer, skel_one, skel_two, near_list, list_one, list_two):
    n_branch, n_sub, n_y = sizes
    n_z = n_branch // n_y
    leaves = leaf_transfer.shape[0]
    window = leaves + 2 * RIM
    rim = RIM * LEAF
    operands = (
        vectors, coords, basis, leaf_transfer, node_transfer, skel_one,
        jnp.transpose(skel_two, (1, 2, 0)), near_list.T, list_one, list_two,
    )
    held = [pltpu.VMEM(a.shape, F32) for a in operands[:7]] + [pltpu.SMEM(operands[7].shape, jnp.int32)]
    held += [pltpu.VMEM(a.shape, jnp.int32) for a in operands[8:]]
    return pl.pallas_call(
        functools.partial(kernel, sizes),
        out_shape=jax.ShapeDtypeStruct(vectors.shape, F32),
        in_specs=[pl.BlockSpec(memory_space=pltpu.HBM)] * 10,
        out_specs=pl.BlockSpec(memory_space=pltpu.HBM),
        scratch_shapes=[
            *held,
            pltpu.VMEM(vectors.shape, F32),
            pltpu.VMEM((2, NV, rim), F32),
            pltpu.VMEM((2, 2, rim), F32),
            pltpu.VMEM((window, 2 * NV, LEAF), BF16),
            pltpu.VMEM((window, LEAF, FEATURES), BF16),
            pltpu.VMEM((FEATURES, leaves * LEAF), BF16),
            pltpu.VMEM((3 * RANK, leaves * LEAF), BF16),
            pltpu.VMEM((n_branch, 2 * RANK), F32),
            pltpu.VMEM((n_y, 1, 128), F32),
            pltpu.VMEM((n_z, 9, 128), F32),
            pltpu.VMEM((n_z, RANK // 2, 128), F32),
            pltpu.VMEM((2 * n_y * RANK, 3 * n_z * RANK), BF16),
            pltpu.VMEM((n_y, RANK, 128), F32),
            pltpu.VMEM((n_y, RANK, 128), F32),
            pltpu.VMEM((RANK, 128), F32),
            pltpu.VMEM((n_sub, RANK // 2, 128), F32),
            pltpu.SemaphoreType.DMA((10,)),
            pltpu.SemaphoreType.DMA((CHUNKS,)),
            pltpu.SemaphoreType.DMA((11,)),
            pltpu.SemaphoreType.DMA((11,)),
            pltpu.SemaphoreType.REGULAR,
        ],
        compiler_params=pltpu.CompilerParams(
            collective_id=0, has_side_effects=True, vmem_limit_bytes=VMEM_LIMIT
        ),
        name="h2_product",
    )(*operands)


def solution(mesh, y_count=Y_COUNT):
    both = ("branch", "sub")
    return jax.shard_map(
        functools.partial(body, (mesh.shape["branch"], mesh.shape["sub"], y_count)),
        mesh=mesh,
        in_specs=(
            P(None, both),
            P(None, both),
            P(None, both),
            P(both, None, None),
            P(both, None, None),
            P(both, None, None),
            P(),
            P(both, None),
            P(both, None),
            P("branch", None),
        ),
        out_specs=P(None, both),
        check_vma=False,
    )
```

```python
import functools
import math

import jax
import jax.numpy as jnp
from jax import lax
from jax.experimental import pallas as pl
from jax.experimental.pallas import tpu as pltpu
from jax.sharding import PartitionSpec as P

MESH = pl.DeviceIdType.MESH
F32 = jnp.float32
BF16 = jnp.bfloat16
NUGGET = 0.5
LOG2E = math.log2(math.e)
LN2 = math.log(2.0)
SCALE = math.sqrt(3.0) / 0.7 * LOG2E
Y_COUNT = 8
LEAF = 128
RANK = 32
NV = 64
RIM = 8
BLOCK = 8
PAIRS = ((0, 1), (2, 3), (4, 5), (6, 7), (8,))
EXACT = lax.Precision.HIGHEST
CENTRE = 1.5
VMEM_LIMIT = 48 * 2**20
FEATURES = 32
NN, NT, TN = ((1,), (0,)), ((1,), (1,)), ((0,), (0,))


def split(x):
    high = x.astype(BF16)
    return high, (x - high.astype(F32)).astype(BF16)


def split3(x):
    first = x.astype(BF16).astype(F32)
    rest = x - first
    second = rest.astype(BF16).astype(F32)
    return first, second, rest - second


def matern_of(square):
    square = jnp.maximum(square, 1e-30)
    dist = square * lax.rsqrt(square)
    return (dist + LOG2E) * jnp.exp2(-dist)


def features(coords):
    w = (coords - CENTRE) * SCALE
    norm = w[0:1] * w[0:1] + w[1:2] * w[1:2]
    s1, s2, s3 = split3(w)
    norms = split3(norm)
    ones = [jnp.ones_like(norm)] * 3
    zeros = jnp.zeros((FEATURES - 18, w.shape[1]), F32)
    t1, t2, t3 = -2.0 * s1, -2.0 * s2, -2.0 * s3
    source = jnp.concatenate([s1, s1, s2, s2, s1, s3, *norms, *ones, zeros], 0)
    target = jnp.concatenate([t1, t2, t1, t2, t3, t1, *ones, *norms, zeros], 0)
    return source, target


def dot_f32(a, b, dims=NN):
    return lax.dot_general(a, b, (dims, ((), ())), precision=EXACT, preferred_element_type=F32)


def dot_high(a, b, dims=NN):
    return lax.dot_general(a, b, (dims, ((), ())), precision=lax.Precision.HIGH, preferred_element_type=F32)


def dot_bf16(a, b, dims=NN):
    return lax.dot_general(a, b, (dims, ((), ())), preferred_element_type=F32)


def fold(r):
    half = r.shape[0] // 2, r.shape[1] // 2
    return r[: half[0], : half[1]] + r[half[0] :, : half[1]] + r[: half[0], half[1] :] + r[half[0] :, half[1] :]


def leaf_cols(i):
    return pl.ds(pl.multiple_of(i * LEAF, LEAF), LEAF)


def kernel(sizes, *refs):
    operands, out = refs[:10], refs[10]
    vec, crd, bas, ltr, ntr, sk1, sk2, near, list1, list2 = refs[11:21]
    hv, hc, vw, fs, ft, w3, sk2t, info, early, column, places, group_tile, mix, part, parts, own_field, fc, load, send, recv, later = refs[21:]
    n_branch, n_sub, n_y = sizes
    n_z = n_branch // n_y
    leaves = ltr.shape[0]
    ny1, nz1, ns1 = pl.ds(1, n_y - 1), pl.ds(1, n_z - 1), pl.ds(1, n_sub - 1)
    b = lax.axis_index("branch")
    s = lax.axis_index("sub")
    z = b // n_y
    y = b % n_y

    loads = [pltpu.make_async_copy(operands[k], refs[11 + k], load.at[k]) for k in range(10)]
    l_vec, l_crd, l_bas, l_ltr, l_ntr, l_sk1, l_sk2, l_near, l_list1, l_list2 = loads
    for copy in (l_ltr, l_bas, l_vec, l_crd, l_ntr, l_sk1, l_sk2, l_near, l_list1, l_list2):
        copy.start()

    def y_peer(d):
        return z * n_y + (y + d) % n_y, s

    def z_peer(d):
        return ((z + d) % n_z) * n_y + y, s

    def sub_peer(d):
        return b, (s + d) % n_sub

    def remote(src, dst, k, peer):
        return pltpu.make_async_remote_copy(
            src_ref=src, dst_ref=dst, send_sem=send.at[k], recv_sem=recv.at[k], device_id=peer, device_id_type=MESH
        )

    def signal(sem, peer):
        pl.semaphore_signal(sem, inc=1, device_id=peer, device_id_type=MESH)

    ys, zs, ss = (sorted(range(1, n), key=lambda d: (-min(d, n - d), d)) for n in (n_y, n_z, n_sub))
    has_lower, has_upper = b > 0, b < n_branch - 1
    lower, upper = (b - 1, s), (b + 1, s)

    barrier = pltpu.get_barrier_semaphore()
    pl.when(has_lower)(lambda: signal(barrier, lower))
    pl.when(has_upper)(lambda: signal(barrier, upper))
    for d in ss:
        signal(barrier, sub_peer(d))
    for d in ys:
        signal(barrier, y_peer(d))
    for other in range(1, n_z):
        pl.when(other > z)(lambda other=other: signal(barrier, (other * n_y + y, s)))

    starts_late = z >= n_z // 2
    met = n_sub - 1 + n_y - 1 + z + has_lower.astype(jnp.int32) + has_upper.astype(jnp.int32)

    def along_z(ref, k, higher):
        for d in zs:
            pl.when(z + d < n_z if higher else z + d >= n_z)(
                lambda d=d: remote(ref.at[0], ref.at[d], k, z_peer(d)).start()
            )

    def enter():
        pl.semaphore_wait(barrier, met)
        for other in range(n_z - 1):
            pl.when(other < z)(lambda other=other: signal(later, (other * n_y + y, s)))
        l_sk1.wait()
        l_list1.wait()
        l_list2.wait()
        l_ntr.wait()
        row = [sk1[0, 0:1], sk1[0, 1:2], list1[...].astype(F32), list2[...].astype(F32)]
        row = jnp.concatenate(row + [jnp.zeros((1, 128 - 2 * RANK - 16), F32)], 1)
        info[0] = row
        early[0, 8:9] = row
        early[0, 0:8] = jnp.concatenate([ntr[0, 8 * k : 8 * (k + 1)] for k in range(4)], 1)
        for d in ys:
            remote(info.at[0], info.at[d], 4, y_peer(d)).start()
        along_z(early, 8, False)

    for side, missing in ((0, b == 0), (1, b == n_branch - 1)):

        @pl.when(missing)
        def _(side=side):
            hv[side] = jnp.zeros(hv.shape[1:], F32)
            hc[side] = jnp.zeros(hc.shape[1:], F32)

    l_ltr.wait()
    l_bas.wait()

    def make_w(i, c):
        cols = leaf_cols(i)
        bh, bl = split(bas[:, cols])
        lh, ll = split(ltr[i])
        w = dot_bf16(jnp.concatenate([lh, lh, ll], 0), jnp.concatenate([bh, bl, bh], 0), TN)
        wh, wl = split(w)
        w3[:RANK, cols] = wh
        w3[RANK : 2 * RANK, cols] = wl
        w3[2 * RANK :, cols] = wh
        return c

    lax.fori_loop(0, leaves, make_w, 0, unroll=16)

    l_vec.wait()

    def own_vectors(i, c):
        high, low = split(vec[:, leaf_cols(i)] * LN2)
        vw[RIM + i, :NV] = high
        vw[RIM + i, NV:] = low
        return c

    lax.fori_loop(0, leaves, own_vectors, 0, unroll=8)
    pl.when(starts_late)(enter)
    own = jnp.concatenate([vw[RIM + i] for i in range(leaves)], 1)
    coeff_t = fold(dot_bf16(own, w3[: 2 * RANK], NT)) * (1.0 / LN2)
    coeff = coeff_t.T
    column[0] = jnp.concatenate([coeff[: RANK // 2], coeff[RANK // 2 :]], 1)
    pl.when(jnp.logical_not(starts_late))(enter)
    along_z(column, 5, False)

    rim = RIM * LEAF
    first, last = pl.ds(0, rim), pl.ds(leaves * LEAF - rim, rim)
    top, bottom = pl.ds(0, NV // 2), pl.ds(NV // 2, NV // 2)
    down = [
        remote(crd.at[:, first], hc.at[1], 0, lower),
        remote(vec.at[top, first], hv.at[1, top], 2, lower),
        remote(vec.at[bottom, first], hv.at[1, bottom], 9, lower),
    ]
    up = [
        remote(crd.at[:, last], hc.at[0], 1, upper),
        remote(vec.at[top, last], hv.at[0, top], 3, upper),
        remote(vec.at[bottom, last], hv.at[0, bottom], 10, upper),
    ]

    def start_all(copies):
        for copy in copies:
            copy.start()

    lower_early = has_lower & jnp.logical_not(starts_late & (y == 0))
    upper_early = has_upper & jnp.logical_not(starts_late & (y == n_y - 1))
    lower_late = has_lower & starts_late & (y == 0)
    upper_late = has_upper & starts_late & (y == n_y - 1)

    l_crd.wait()
    pl.when(lower_early)(lambda: start_all(down))
    pl.when(upper_early)(lambda: start_all(up))
    wide = 8 * LEAF

    def own_features(i, c):
        cols = pl.ds(pl.multiple_of(i * wide, wide), wide)
        source, target = features(crd[:, cols])
        ft[:, cols] = target.astype(BF16)
        flat = source.T.astype(BF16)
        for k in range(8):
            fs[RIM + i * 8 + k] = flat[k * LEAF : (k + 1) * LEAF]
        return c

    lax.fori_loop(0, leaves // 8, own_features, 0)
    l_sk2.wait()
    sk2t[...] = jnp.concatenate([sk2[0].T, sk2[1].T], 1)

    def source_names(scale, offset):
        names = []
        for d in range(n_z):
            name = ((z + n_z - d) % n_z * n_y + y) * scale + offset
            names.append(jnp.full((1, RANK), name.astype(F32), F32))
        return jnp.concatenate(names, 1)

    def counted_tile(at, target, source, names, lane):
        sx = jnp.concatenate([r[:, :RANK] for r in source], 1) * SCALE
        sy = jnp.concatenate([r[:, RANK : 2 * RANK] for r in source], 1) * SCALE
        dx = at[:, 0:1] - sx
        dy = at[:, 1:2] - sy
        count = jnp.zeros((n_y, n_z * RANK), F32)
        for k in range(8):
            count = count + (target[:, lane + k : lane + k + 1] == names).astype(F32)
        count = jnp.concatenate([jnp.broadcast_to(count[d : d + 1], (RANK, n_z * RANK)) for d in range(n_y)], 0)
        return matern_of(dx * dx + dy * dy) * (count * LN2)

    def targets():
        return jnp.concatenate([info[(n_y - d) % n_y] for d in range(n_y)], 0)

    def keep_mix(level, tile):
        high, low = split(tile)
        mix[level * n_y * RANK : (level + 1) * n_y * RANK] = jnp.concatenate([high, high, low], 1)

    def prepare_groups():
        remote(info.at[ny1], info.at[ny1], 4, y_peer(1)).wait_recv()
        target = targets()
        group = [sk2t[pl.ds(z * n_y + (y + d) % n_y, 1)] for d in range(n_y)]
        line = [jnp.concatenate([target[d : d + 1, RANK * k : RANK * (k + 1)] for d in range(n_y)], 1) for k in range(2)]
        line += [jnp.concatenate([g[:, RANK * k : RANK * (k + 1)] for g in group], 1) for k in range(2)]
        at = (jnp.concatenate(line + [jnp.zeros((4, n_y * RANK), F32)], 0) * SCALE).T
        places[...] = at
        group_rows = [sk2t[pl.ds((z + n_z - d) % n_z * n_y + y, 1)] for d in range(n_z)]
        group_tile[...] = counted_tile(at[:, 2:4], target, group_rows, source_names(1, 0), 2 * RANK + 8)

    pl.when(z < n_z // 2)(prepare_groups)

    @pl.when(z < n_z - 1)
    def _():
        pl.semaphore_wait(later, n_z - 1 - z)

    along_z(early, 8, True)
    along_z(column, 5, True)
    pl.when(lower_late)(lambda: start_all(down[:2]))
    @pl.when(starts_late)
    def _():
        prepare_groups()
        pl.when(lower_late)(lambda: start_all(down[2:]))
        pl.when(upper_late)(lambda: start_all(up))

    def prepare_nodes():
        remote(early.at[nz1], early.at[nz1], 8, z_peer(1)).wait_recv()
        moved = []
        for d in range(n_z):
            transfer = jnp.concatenate([early[d, 0:8, RANK * k : RANK * (k + 1)] for k in range(4)], 0)
            moved.append(dot_high(group_tile[:, d * RANK : (d + 1) * RANK], transfer, NT))
        keep_mix(1, jnp.concatenate(moved, 1))
        node_rows = [early[d, 8:9] for d in range(n_z)]
        keep_mix(0, counted_tile(places[:, 0:2], targets(), node_rows, source_names(n_sub, s), 2 * RANK))

    def send_parts():
        remote(column.at[nz1], column.at[nz1], 5, z_peer(1)).wait_recv()
        coeffs = []
        for d in range(n_z):
            coeffs += [column[d, :, :NV], column[d, :, NV:]]
        high, low = split(jnp.concatenate(coeffs, 0))
        fields = dot_bf16(mix[...], jnp.concatenate([high, low, high], 0))
        for d in range(n_y):
            at = d * RANK
            part[d] = jnp.concatenate([fields[at : at + RANK], fields[n_y * RANK + at : n_y * RANK + at + RANK]], 1)
        for d in ys:
            remote(part.at[d], parts.at[d], 6, y_peer(d)).start()

    def both_parts():
        prepare_nodes()
        send_parts()

    in_second_half = z >= n_z // 2 - 1
    parts_first = in_second_half | (y == n_y - 1)
    pl.when(parts_first)(both_parts)
    l_near.wait()

    def arrived(copies):
        for copy in copies:
            copy.wait_recv()

    def rims(waits, take):
        for side, there, copies in ((0, has_lower, up), (1, has_upper, down)):
            pl.when(there)(lambda copies=copies: arrived(copies[waits]))
            take(side, side * (RIM + leaves))

    def rim_features(side, base):
        source, _ = features(hc[side])
        flat = source.T.astype(BF16)
        for k in range(RIM):
            fs[base + k] = flat[k * LEAF : (k + 1) * LEAF]

    def rim_vectors(side, base):
        for i in range(RIM):
            high, low = split(hv[side, :, i * LEAF : (i + 1) * LEAF] * LN2)
            vw[base + i, :NV] = high
            vw[base + i, NV:] = low

    rims(slice(0, 1), rim_features)
    rims(slice(1, 3), rim_vectors)

    def near_leaves(first_leaf):
        items = [(first_leaf + u, pair) for u in range(BLOCK) for pair in PAIRS]

        def slots(i, pair):
            found = []
            for j in pair:
                named = near[j, i]
                slot = (named // (n_sub * leaves) - b) * leaves + named % leaves + RIM
                found.append(jnp.clip(slot, 0, leaves + 2 * RIM - 1))
            return found

        squares, tiles, acc = {}, {}, None
        for step in range(len(items) + 2):
            if step < len(items):
                i, pair = items[step]
                named = slots(i, pair)
                sources = jnp.concatenate([fs[m] for m in named], 0)
                squares[step] = named, dot_bf16(sources, ft[:, leaf_cols(i)])
            if 0 <= step - 1 < len(items):
                named, square = squares.pop(step - 1)
                tiles[step - 1] = named, jnp.concatenate(split(matern_of(square)), 1)
            if step >= 2:
                i, pair = items[step - 2]
                named, tile = tiles.pop(step - 2)
                part = dot_bf16(jnp.concatenate([vw[m] for m in named], 1), tile)
                acc = part if acc is None else acc + part
                if pair == PAIRS[-1]:
                    out[:, leaf_cols(i)] = fold(acc) + NUGGET * vec[:, leaf_cols(i)]
                    acc = None

    def send_group():
        remote(parts.at[ny1], parts.at[ny1], 6, y_peer(1)).wait_recv()
        field = part[0]
        for d in ys:
            field = field + parts[d]
        own_field[...] = field
        fc[0] = jnp.concatenate([field[: RANK // 2, NV:], field[RANK // 2 :, NV:]], 1)
        for d in ss:
            remote(fc.at[0], fc.at[d], 7, sub_peer(d)).start()

    parts_step = jnp.where(parts_first, leaves // BLOCK, 1)
    group_step = jnp.where(in_second_half, 2, 3)

    def near_block(t, c):
        pl.when(t == parts_step)(both_parts)
        pl.when(t == group_step)(send_group)
        near_leaves(t * BLOCK)
        return c

    lax.fori_loop(0, leaves // BLOCK, near_block, 0)

    remote(fc.at[ns1], fc.at[ns1], 7, sub_peer(1)).wait_recv()
    group = fc[0]
    for d in ss:
        group = group + fc[d]
    group = jnp.concatenate([group[:, :NV], group[:, NV:]], 0)
    field = own_field[:, :NV] + dot_high(ntr[0], group)
    fh, fl = split(field.T)
    lhs = jnp.concatenate([fh, fh, fl], 1)

    for i in range(leaves // 2):
        cols = pl.ds(i * 2 * LEAF, 2 * LEAF)
        out[:, cols] += dot_bf16(lhs, w3[:, cols])

    def finish(copies):
        for copy in copies:
            copy.wait_send()

    pl.when(has_lower)(lambda: finish(down))
    pl.when(has_upper)(lambda: finish(up))
    for ref, k in ((info.at[ny1], 4), (column.at[nz1], 5), (parts.at[ny1], 6), (fc.at[ns1], 7), (early.at[nz1], 8)):
        remote(ref, ref, k, sub_peer(1)).wait_send()


def body(sizes, vectors, coords, basis, leaf_transfer, node_transfer, skel_one, skel_two, near_list, list_one, list_two):
    n_branch, n_sub, n_y = sizes
    n_z = n_branch // n_y
    leaves = leaf_transfer.shape[0]
    window = leaves + 2 * RIM
    rim = RIM * LEAF
    operands = (
        vectors, coords, basis, leaf_transfer, node_transfer, skel_one,
        jnp.transpose(skel_two, (1, 2, 0)), near_list.T, list_one, list_two,
    )
    held = [pltpu.VMEM(a.shape, F32) for a in operands[:7]] + [pltpu.SMEM(operands[7].shape, jnp.int32)]
    held += [pltpu.VMEM(a.shape, jnp.int32) for a in operands[8:]]
    return pl.pallas_call(
        functools.partial(kernel, sizes),
        out_shape=pltpu.VMEM(vectors.shape, F32),
        in_specs=[pl.BlockSpec(memory_space=pltpu.HBM)] * 10,
        out_specs=pl.BlockSpec(memory_space=pltpu.VMEM),
        scratch_shapes=[
            *held,
            pltpu.VMEM((2, NV, rim), F32),
            pltpu.VMEM((2, 2, rim), F32),
            pltpu.VMEM((window, 2 * NV, LEAF), BF16),
            pltpu.VMEM((window, LEAF, FEATURES), BF16),
            pltpu.VMEM((FEATURES, leaves * LEAF), BF16),
            pltpu.VMEM((3 * RANK, leaves * LEAF), BF16),
            pltpu.VMEM((n_branch, 2 * RANK), F32),
            pltpu.VMEM((n_y, 1, 128), F32),
            pltpu.VMEM((n_z, 9, 128), F32),
            pltpu.VMEM((n_z, RANK // 2, 128), F32),
            pltpu.VMEM((n_y * RANK, 8), F32),
            pltpu.VMEM((n_y * RANK, n_z * RANK), F32),
            pltpu.VMEM((2 * n_y * RANK, 3 * n_z * RANK), BF16),
            pltpu.VMEM((n_y, RANK, 128), F32),
            pltpu.VMEM((n_y, RANK, 128), F32),
            pltpu.VMEM((RANK, 128), F32),
            pltpu.VMEM((n_sub, RANK // 2, 128), F32),
            pltpu.SemaphoreType.DMA((10,)),
            pltpu.SemaphoreType.DMA((11,)),
            pltpu.SemaphoreType.DMA((11,)),
            pltpu.SemaphoreType.REGULAR,
        ],
        compiler_params=pltpu.CompilerParams(
            collective_id=0, has_side_effects=True, vmem_limit_bytes=VMEM_LIMIT
        ),
        name="h2_product",
    )(*[pltpu.with_memory_space_constraint(a, pltpu.HBM) for a in operands])


def solution(mesh, y_count=Y_COUNT):
    both = ("branch", "sub")
    return jax.shard_map(
        functools.partial(body, (mesh.shape["branch"], mesh.shape["sub"], y_count)),
        mesh=mesh,
        in_specs=(
            P(None, both),
            P(None, both),
            P(None, both),
            P(both, None, None),
            P(both, None, None),
            P(both, None, None),
            P(),
            P(both, None),
            P(both, None),
            P("branch", None),
        ),
        out_specs=P(None, both),
        check_vma=False,
    )
```

```python
import functools
import math

import jax
import jax.numpy as jnp
from jax import lax
from jax.experimental import pallas as pl
from jax.experimental.pallas import tpu as pltpu
from jax.sharding import PartitionSpec as P

MESH = pl.DeviceIdType.MESH
F32 = jnp.float32
BF16 = jnp.bfloat16
NUGGET = 0.5
LOG2E = math.log2(math.e)
LN2 = math.log(2.0)
SCALE = math.sqrt(3.0) / 0.7 * LOG2E
Y_COUNT = 8
LEAF = 128
RANK = 32
NV = 64
RIM = 8
BLOCK = 8
PAIRS = ((0, 1), (2, 3), (4, 5), (6, 7), (8,))
EXACT = lax.Precision.HIGHEST
CENTRE = 1.5
VMEM_LIMIT = 48 * 2**20
FEATURES = 32
NN, NT, TN = ((1,), (0,)), ((1,), (1,)), ((0,), (0,))


def split(x):
    high = x.astype(BF16)
    return high, (x - high.astype(F32)).astype(BF16)


def split3(x):
    first = x.astype(BF16).astype(F32)
    rest = x - first
    second = rest.astype(BF16).astype(F32)
    return first, second, rest - second


def matern_of(square):
    square = jnp.maximum(square, 1e-30)
    dist = square * lax.rsqrt(square)
    return (dist + LOG2E) * jnp.exp2(-dist)


def features(coords):
    w = (coords - CENTRE) * SCALE
    norm = w[0:1] * w[0:1] + w[1:2] * w[1:2]
    s1, s2, s3 = split3(w)
    norms = split3(norm)
    ones = [jnp.ones_like(norm)] * 3
    zeros = jnp.zeros((FEATURES - 18, w.shape[1]), F32)
    t1, t2, t3 = -2.0 * s1, -2.0 * s2, -2.0 * s3
    source = jnp.concatenate([s1, s1, s2, s2, s1, s3, *norms, *ones, zeros], 0)
    target = jnp.concatenate([t1, t2, t1, t2, t3, t1, *ones, *norms, zeros], 0)
    return source, target


def dot_f32(a, b, dims=NN):
    return lax.dot_general(a, b, (dims, ((), ())), precision=EXACT, preferred_element_type=F32)


def dot_high(a, b, dims=NN):
    return lax.dot_general(a, b, (dims, ((), ())), precision=lax.Precision.HIGH, preferred_element_type=F32)


def dot_bf16(a, b, dims=NN):
    return lax.dot_general(a, b, (dims, ((), ())), preferred_element_type=F32)


def fold(r):
    half = r.shape[0] // 2, r.shape[1] // 2
    return r[: half[0], : half[1]] + r[half[0] :, : half[1]] + r[: half[0], half[1] :] + r[half[0] :, half[1] :]


def leaf_cols(i):
    return pl.ds(pl.multiple_of(i * LEAF, LEAF), LEAF)


def kernel(sizes, *refs):
    operands, out = refs[:10], refs[10]
    vec, crd, bas, ltr, ntr, sk1, sk2, near, list1, list2 = refs[11:21]
    hv, hc, vw, fs, ft, w3, sk2t, info, early, column, places, group_tile, mix, group_part, group_parts, node_part, node_parts, fc, load, send, recv, later = refs[21:]
    n_branch, n_sub, n_y = sizes
    n_z = n_branch // n_y
    leaves = ltr.shape[0]
    ny1, nz1, ns1 = pl.ds(1, n_y - 1), pl.ds(1, n_z - 1), pl.ds(1, n_sub - 1)
    b = lax.axis_index("branch")
    s = lax.axis_index("sub")
    z = b // n_y
    y = b % n_y

    loads = [pltpu.make_async_copy(operands[k], refs[11 + k], load.at[k]) for k in range(10)]
    l_vec, l_crd, l_bas, l_ltr, l_ntr, l_sk1, l_sk2, l_near, l_list1, l_list2 = loads
    l_ltr.start()
    l_bas.start()

    def y_peer(d):
        return z * n_y + (y + d) % n_y, s

    def z_peer(d):
        return ((z + d) % n_z) * n_y + y, s

    def sub_peer(d):
        return b, (s + d) % n_sub

    def remote(src, dst, k, peer):
        return pltpu.make_async_remote_copy(
            src_ref=src, dst_ref=dst, send_sem=send.at[k], recv_sem=recv.at[k], device_id=peer, device_id_type=MESH
        )

    def signal(sem, peer):
        pl.semaphore_signal(sem, inc=1, device_id=peer, device_id_type=MESH)

    ys, zs, ss = (sorted(range(1, n), key=lambda d: (-min(d, n - d), d)) for n in (n_y, n_z, n_sub))
    has_lower, has_upper = b > 0, b < n_branch - 1
    lower, upper = (b - 1, s), (b + 1, s)

    barrier = pltpu.get_barrier_semaphore()
    pl.when(has_lower)(lambda: signal(barrier, lower))
    pl.when(has_upper)(lambda: signal(barrier, upper))
    for d in ss:
        signal(barrier, sub_peer(d))
    for d in ys:
        signal(barrier, y_peer(d))
    for other in range(1, n_z):
        pl.when(other > z)(lambda other=other: signal(barrier, (other * n_y + y, s)))

    starts_late = z >= n_z // 2
    met = n_sub - 1 + n_y - 1 + z + has_lower.astype(jnp.int32) + has_upper.astype(jnp.int32)

    def along_z(ref, k, higher):
        for d in zs:
            pl.when(z + d < n_z if higher else z + d >= n_z)(
                lambda d=d: remote(ref.at[0], ref.at[d], k, z_peer(d)).start()
            )

    def enter():
        pl.semaphore_wait(barrier, met)
        for other in range(n_z - 1):
            pl.when(other < z)(lambda other=other: signal(later, (other * n_y + y, s)))
        l_sk1.wait()
        l_list1.wait()
        l_list2.wait()
        l_ntr.wait()
        row = [sk1[0, 0:1], sk1[0, 1:2], list1[...].astype(F32), list2[...].astype(F32)]
        row = jnp.concatenate(row + [jnp.zeros((1, 128 - 2 * RANK - 16), F32)], 1)
        info[0] = row
        early[0, 8:9] = row
        early[0, 0:8] = jnp.concatenate([ntr[0, 8 * k : 8 * (k + 1)] for k in range(4)], 1)
        for d in ys:
            remote(info.at[0], info.at[d], 4, y_peer(d)).start()
        along_z(early, 8, False)

    for copy in (l_vec, l_ntr, l_sk1, l_list1, l_list2, l_crd, l_sk2, l_near):
        copy.start()

    for side, missing in ((0, b == 0), (1, b == n_branch - 1)):

        @pl.when(missing)
        def _(side=side):
            hv[side] = jnp.zeros(hv.shape[1:], F32)
            hc[side] = jnp.zeros(hc.shape[1:], F32)

    l_ltr.wait()
    l_bas.wait()

    def make_w(i, c):
        cols = leaf_cols(i)
        bh, bl = split(bas[:, cols])
        lh, ll = split(ltr[i])
        w = dot_bf16(jnp.concatenate([lh, lh, ll], 0), jnp.concatenate([bh, bl, bh], 0), TN)
        wh, wl = split(w)
        w3[:RANK, cols] = wh
        w3[RANK : 2 * RANK, cols] = wl
        w3[2 * RANK :, cols] = wh
        return c

    lax.fori_loop(0, leaves, make_w, 0, unroll=16)

    l_vec.wait()

    def own_vectors(i, c):
        high, low = split(vec[:, leaf_cols(i)] * LN2)
        vw[RIM + i, :NV] = high
        vw[RIM + i, NV:] = low
        return c

    lax.fori_loop(0, leaves, own_vectors, 0, unroll=8)
    enters_first = starts_late & (y >= 2) & (y <= n_y - 2)
    pl.when(enters_first)(enter)
    own = jnp.concatenate([vw[RIM + i] for i in range(leaves)], 1)
    coeff_t = fold(dot_bf16(own, w3[: 2 * RANK], NT)) * (1.0 / LN2)
    coeff = coeff_t.T
    column[0] = jnp.concatenate([coeff[: RANK // 2], coeff[RANK // 2 :]], 1)
    pl.when(jnp.logical_not(enters_first))(enter)
    along_z(column, 5, False)

    rim = RIM * LEAF
    first, last = pl.ds(0, rim), pl.ds(leaves * LEAF - rim, rim)
    top, bottom = pl.ds(0, NV // 2), pl.ds(NV // 2, NV // 2)
    down = [
        remote(crd.at[:, first], hc.at[1], 0, lower),
        remote(vec.at[top, first], hv.at[1, top], 2, lower),
        remote(vec.at[bottom, first], hv.at[1, bottom], 9, lower),
    ]
    up = [
        remote(crd.at[:, last], hc.at[0], 1, upper),
        remote(vec.at[top, last], hv.at[0, top], 3, upper),
        remote(vec.at[bottom, last], hv.at[0, bottom], 10, upper),
    ]

    def start_all(copies):
        for copy in copies:
            copy.start()

    upper_early = has_upper & jnp.logical_not(starts_late & (y == n_y - 1))
    upper_late = has_upper & starts_late & (y == n_y - 1)

    l_crd.wait()
    pl.when(has_lower)(lambda: start_all(down))
    pl.when(upper_early)(lambda: start_all(up))
    wide = 8 * LEAF

    def own_features(i, c):
        cols = pl.ds(pl.multiple_of(i * wide, wide), wide)
        source, target = features(crd[:, cols])
        ft[:, cols] = target.astype(BF16)
        flat = source.T.astype(BF16)
        for k in range(8):
            fs[RIM + i * 8 + k] = flat[k * LEAF : (k + 1) * LEAF]
        return c

    lax.fori_loop(0, leaves // 8, own_features, 0)
    l_sk2.wait()
    sk2t[...] = jnp.concatenate([sk2[0].T, sk2[1].T], 1)

    def source_names(scale, offset):
        names = []
        for d in range(n_z):
            name = ((z + n_z - d) % n_z * n_y + y) * scale + offset
            names.append(jnp.full((1, RANK), name.astype(F32), F32))
        return jnp.concatenate(names, 1)

    def counted_tile(at, target, source, names, lane):
        sx = jnp.concatenate([r[:, :RANK] for r in source], 1) * SCALE
        sy = jnp.concatenate([r[:, RANK : 2 * RANK] for r in source], 1) * SCALE
        dx = at[:, 0:1] - sx
        dy = at[:, 1:2] - sy
        count = jnp.zeros((n_y, n_z * RANK), F32)
        for k in range(8):
            count = count + (target[:, lane + k : lane + k + 1] == names).astype(F32)
        count = jnp.concatenate([jnp.broadcast_to(count[d : d + 1], (RANK, n_z * RANK)) for d in range(n_y)], 0)
        return matern_of(dx * dx + dy * dy) * (count * LN2)

    def targets():
        return jnp.concatenate([info[(n_y - d) % n_y] for d in range(n_y)], 0)

    def keep_mix(level, tile):
        high, low = split(tile)
        mix[level * n_y * RANK : (level + 1) * n_y * RANK] = jnp.concatenate([high, high, low], 1)

    def prepare_groups():
        remote(info.at[ny1], info.at[ny1], 4, y_peer(1)).wait_recv()
        target = targets()
        group = [sk2t[pl.ds(z * n_y + (y + d) % n_y, 1)] for d in range(n_y)]
        line = [jnp.concatenate([target[d : d + 1, RANK * k : RANK * (k + 1)] for d in range(n_y)], 1) for k in range(2)]
        line += [jnp.concatenate([g[:, RANK * k : RANK * (k + 1)] for g in group], 1) for k in range(2)]
        at = (jnp.concatenate(line + [jnp.zeros((4, n_y * RANK), F32)], 0) * SCALE).T
        places[...] = at
        group_rows = [sk2t[pl.ds((z + n_z - d) % n_z * n_y + y, 1)] for d in range(n_z)]
        group_tile[...] = counted_tile(at[:, 2:4], target, group_rows, source_names(1, 0), 2 * RANK + 8)

    pl.when(z < n_z // 2)(prepare_groups)

    def send_higher():
        @pl.when(z < n_z - 1)
        def _():
            pl.semaphore_wait(later, n_z - 1 - z)

        along_z(early, 8, True)
        along_z(column, 5, True)

    in_second_half = z >= n_z // 2 - 1
    waits_less = b == 0
    parts_first = in_second_half | (y == n_y - 1)
    parts_step = jnp.where(parts_first, leaves // BLOCK, 1)
    group_step = jnp.where(parts_first | ((b == 0) & (s != 1)), 2, 3)
    pl.when(jnp.logical_not(waits_less))(send_higher)

    @pl.when(starts_late)
    def _():
        prepare_groups()
        pl.when(upper_late)(lambda: start_all(up))

    def prepare_nodes():
        remote(early.at[nz1], early.at[nz1], 8, z_peer(1)).wait_recv()
        moved = []
        for d in range(n_z):
            transfer = jnp.concatenate([early[d, 0:8, RANK * k : RANK * (k + 1)] for k in range(4)], 0)
            moved.append(dot_high(group_tile[:, d * RANK : (d + 1) * RANK], transfer, NT))
        keep_mix(1, jnp.concatenate(moved, 1))
        node_rows = [early[d, 8:9] for d in range(n_z)]
        keep_mix(0, counted_tile(places[:, 0:2], targets(), node_rows, source_names(n_sub, s), 2 * RANK))

    def send_parts():
        remote(column.at[nz1], column.at[nz1], 5, z_peer(1)).wait_recv()
        coeffs = []
        for d in range(n_z):
            coeffs += [column[d, :, :NV], column[d, :, NV:]]
        high, low = split(jnp.concatenate(coeffs, 0))
        coeffs = jnp.concatenate([high, low, high], 0)
        for level, own, k in ((1, group_part, 6), (0, node_part, 11)):
            fields = dot_bf16(mix[level * n_y * RANK : (level + 1) * n_y * RANK], coeffs)
            for d in [*ys, 0]:
                at = d * RANK
                own[d] = jnp.concatenate([fields[at : at + RANK // 2], fields[at + RANK // 2 : at + RANK]], 1)
                if d:
                    remote(own.at[d], (group_parts if level else node_parts).at[d], k, y_peer(d)).start()

    def both_parts():
        prepare_nodes()
        send_parts()

    pl.when(parts_first)(both_parts)
    l_near.wait()

    def arrived(copies):
        for copy in copies:
            copy.wait_recv()

    def rims(waits, take):
        for side, there, copies in ((0, has_lower, up), (1, has_upper, down)):
            pl.when(there)(lambda copies=copies: arrived(copies[waits]))
            take(side, side * (RIM + leaves))

    def rim_features(side, base):
        source, _ = features(hc[side])
        flat = source.T.astype(BF16)
        for k in range(RIM):
            fs[base + k] = flat[k * LEAF : (k + 1) * LEAF]

    def rim_vectors(side, base):
        for i in range(RIM):
            high, low = split(hv[side, :, i * LEAF : (i + 1) * LEAF] * LN2)
            vw[base + i, :NV] = high
            vw[base + i, NV:] = low

    rims(slice(0, 1), rim_features)
    rims(slice(1, 3), rim_vectors)

    def near_leaves(first_leaf):
        items = [(first_leaf + u, pair) for u in range(BLOCK) for pair in PAIRS]

        def slots(i, pair):
            found = []
            for j in pair:
                named = near[j, i]
                slot = (named // (n_sub * leaves) - b) * leaves + named % leaves + RIM
                found.append(jnp.clip(slot, 0, leaves + 2 * RIM - 1))
            return found

        squares, tiles, acc = {}, {}, None
        for step in range(len(items) + 2):
            if step < len(items):
                i, pair = items[step]
                named = slots(i, pair)
                sources = jnp.concatenate([fs[m] for m in named], 0)
                squares[step] = named, dot_bf16(sources, ft[:, leaf_cols(i)])
            if 0 <= step - 1 < len(items):
                named, square = squares.pop(step - 1)
                tiles[step - 1] = named, jnp.concatenate(split(matern_of(square)), 1)
            if step >= 2:
                i, pair = items[step - 2]
                named, tile = tiles.pop(step - 2)
                part = dot_bf16(jnp.concatenate([vw[m] for m in named], 1), tile)
                acc = part if acc is None else acc + part
                if pair == PAIRS[-1]:
                    out[:, leaf_cols(i)] = fold(acc) + NUGGET * vec[:, leaf_cols(i)]
                    acc = None

    def send_group():
        remote(group_parts.at[ny1], group_parts.at[ny1], 6, y_peer(1)).wait_recv()
        field = group_part[0]
        for d in ys:
            field = field + group_parts[d]
        fc[0] = field
        for d in ss:
            remote(fc.at[0], fc.at[d], 7, sub_peer(d)).start()


    def near_block(t, c):
        pl.when((t == 1) & waits_less)(send_higher)
        pl.when(t == parts_step)(both_parts)
        pl.when(t == group_step)(send_group)
        near_leaves(t * BLOCK)
        return c

    lax.fori_loop(0, leaves // BLOCK, near_block, 0)

    def finish(copies):
        for copy in copies:
            copy.wait_send()

    pl.when(has_lower)(lambda: finish(down))
    pl.when(has_upper)(lambda: finish(up))
    for ref, k in (
        (info.at[ny1], 4), (column.at[nz1], 5), (group_parts.at[ny1], 6), (fc.at[ns1], 7), (early.at[nz1], 8),
        (node_parts.at[ny1], 11),
    ):
        remote(ref, ref, k, sub_peer(1)).wait_send()

    remote(node_parts.at[ny1], node_parts.at[ny1], 11, y_peer(1)).wait_recv()
    field = node_part[0]
    for d in ys:
        field = field + node_parts[d]
    own_field = jnp.concatenate([field[:, :NV], field[:, NV:]], 0)
    remote(fc.at[ns1], fc.at[ns1], 7, sub_peer(1)).wait_recv()
    group = fc[0]
    for d in ss:
        group = group + fc[d]
    group = jnp.concatenate([group[:, :NV], group[:, NV:]], 0)
    field = own_field + dot_high(ntr[0], group)
    fh, fl = split(field.T)
    lhs = jnp.concatenate([fh, fh, fl], 1)

    for i in range(leaves // 2):
        cols = pl.ds(i * 2 * LEAF, 2 * LEAF)
        out[:, cols] += dot_bf16(lhs, w3[:, cols])


def body(sizes, vectors, coords, basis, leaf_transfer, node_transfer, skel_one, skel_two, near_list, list_one, list_two):
    n_branch, n_sub, n_y = sizes
    n_z = n_branch // n_y
    leaves = leaf_transfer.shape[0]
    window = leaves + 2 * RIM
    rim = RIM * LEAF
    operands = (
        vectors, coords, basis, leaf_transfer, node_transfer, skel_one,
        jnp.transpose(skel_two, (1, 2, 0)), near_list.T, list_one, list_two,
    )
    held = [pltpu.VMEM(a.shape, F32) for a in operands[:7]] + [pltpu.SMEM(operands[7].shape, jnp.int32)]
    held += [pltpu.VMEM(a.shape, jnp.int32) for a in operands[8:]]
    return pl.pallas_call(
        functools.partial(kernel, sizes),
        out_shape=pltpu.VMEM(vectors.shape, F32),
        in_specs=[pl.BlockSpec(memory_space=pltpu.HBM)] * 10,
        out_specs=pl.BlockSpec(memory_space=pltpu.VMEM),
        scratch_shapes=[
            *held,
            pltpu.VMEM((2, NV, rim), F32),
            pltpu.VMEM((2, 2, rim), F32),
            pltpu.VMEM((window, 2 * NV, LEAF), BF16),
            pltpu.VMEM((window, LEAF, FEATURES), BF16),
            pltpu.VMEM((FEATURES, leaves * LEAF), BF16),
            pltpu.VMEM((3 * RANK, leaves * LEAF), BF16),
            pltpu.VMEM((n_branch, 2 * RANK), F32),
            pltpu.VMEM((n_y, 1, 128), F32),
            pltpu.VMEM((n_z, 9, 128), F32),
            pltpu.VMEM((n_z, RANK // 2, 128), F32),
            pltpu.VMEM((n_y * RANK, 8), F32),
            pltpu.VMEM((n_y * RANK, n_z * RANK), F32),
            pltpu.VMEM((2 * n_y * RANK, 3 * n_z * RANK), BF16),
            pltpu.VMEM((n_y, RANK // 2, 128), F32),
            pltpu.VMEM((n_y, RANK // 2, 128), F32),
            pltpu.VMEM((n_y, RANK // 2, 128), F32),
            pltpu.VMEM((n_y, RANK // 2, 128), F32),
            pltpu.VMEM((n_sub, RANK // 2, 128), F32),
            pltpu.SemaphoreType.DMA((10,)),
            pltpu.SemaphoreType.DMA((12,)),
            pltpu.SemaphoreType.DMA((12,)),
            pltpu.SemaphoreType.REGULAR,
        ],
        compiler_params=pltpu.CompilerParams(
            collective_id=0, has_side_effects=True, vmem_limit_bytes=VMEM_LIMIT
        ),
        name="h2_product",
    )(*[pltpu.with_memory_space_constraint(a, pltpu.HBM) for a in operands])


def solution(mesh, y_count=Y_COUNT):
    both = ("branch", "sub")
    return jax.shard_map(
        functools.partial(body, (mesh.shape["branch"], mesh.shape["sub"], y_count)),
        mesh=mesh,
        in_specs=(
            P(None, both),
            P(None, both),
            P(None, both),
            P(both, None, None),
            P(both, None, None),
            P(both, None, None),
            P(),
            P(both, None),
            P(both, None),
            P("branch", None),
        ),
        out_specs=P(None, both),
        check_vma=False,
    )
```

```python
import functools
import math

import jax
import jax.numpy as jnp
from jax import lax
from jax.experimental import pallas as pl
from jax.experimental.pallas import tpu as pltpu
from jax.sharding import PartitionSpec as P

MESH = pl.DeviceIdType.MESH
F32 = jnp.float32
BF16 = jnp.bfloat16
NUGGET = 0.5
LOG2E = math.log2(math.e)
LN2 = math.log(2.0)
SCALE = math.sqrt(3.0) / 0.7 * LOG2E
Y_COUNT = 8
LEAF = 128
RANK = 32
NV = 64
RIM = 8
BLOCK = 8
PAIRS = ((0, 1), (2, 3), (4, 5), (6, 7), (8,))
EXACT = lax.Precision.HIGHEST
CENTRE = 1.5
VMEM_LIMIT = 48 * 2**20
FEATURES = 32
NN, NT, TN = ((1,), (0,)), ((1,), (1,)), ((0,), (0,))


def split(x):
    high = x.astype(BF16)
    return high, (x - high.astype(F32)).astype(BF16)


def split3(x):
    first = x.astype(BF16).astype(F32)
    rest = x - first
    second = rest.astype(BF16).astype(F32)
    return first, second, rest - second


def matern_of(square):
    square = jnp.maximum(square, 1e-30)
    dist = square * lax.rsqrt(square)
    return (dist + LOG2E) * jnp.exp2(-dist)


def features(coords):
    w = (coords - CENTRE) * SCALE
    norm = w[0:1] * w[0:1] + w[1:2] * w[1:2]
    s1, s2, s3 = split3(w)
    norms = split3(norm)
    ones = [jnp.ones_like(norm)] * 3
    zeros = jnp.zeros((FEATURES - 18, w.shape[1]), F32)
    t1, t2, t3 = -2.0 * s1, -2.0 * s2, -2.0 * s3
    source = jnp.concatenate([s1, s1, s2, s2, s1, s3, *norms, *ones, zeros], 0)
    target = jnp.concatenate([t1, t2, t1, t2, t3, t1, *ones, *norms, zeros], 0)
    return source, target


def dot_f32(a, b, dims=NN):
    return lax.dot_general(a, b, (dims, ((), ())), precision=EXACT, preferred_element_type=F32)


def dot_high(a, b, dims=NN):
    return lax.dot_general(a, b, (dims, ((), ())), precision=lax.Precision.HIGH, preferred_element_type=F32)


def dot_bf16(a, b, dims=NN):
    return lax.dot_general(a, b, (dims, ((), ())), preferred_element_type=F32)


def fold(r):
    half = r.shape[0] // 2, r.shape[1] // 2
    return r[: half[0], : half[1]] + r[half[0] :, : half[1]] + r[: half[0], half[1] :] + r[half[0] :, half[1] :]


def leaf_cols(i):
    return pl.ds(pl.multiple_of(i * LEAF, LEAF), LEAF)


def kernel(sizes, *refs):
    operands, out = refs[:10], refs[10]
    vec, crd, bas, ltr, ntr, sk1, sk2, near, list1, list2 = refs[11:21]
    hv, hc, vw, fs, ft, w3, sk2t, info, early, column, places, group_tile, mix, group_part, group_parts, node_part, node_parts, fc, load, send, recv, later = refs[21:]
    n_branch, n_sub, n_y = sizes
    n_z = n_branch // n_y
    leaves = ltr.shape[0]
    ny1, nz1, ns1 = pl.ds(1, n_y - 1), pl.ds(1, n_z - 1), pl.ds(1, n_sub - 1)
    b = lax.axis_index("branch")
    s = lax.axis_index("sub")
    z = b // n_y
    y = b % n_y

    loads = [pltpu.make_async_copy(operands[k], refs[11 + k], load.at[k]) for k in range(10)]
    l_vec, l_crd, l_bas, l_ltr, l_ntr, l_sk1, l_sk2, l_near, l_list1, l_list2 = loads
    l_ltr.start()
    l_bas.start()

    def y_peer(d):
        return z * n_y + (y + d) % n_y, s

    def z_peer(d):
        return ((z + d) % n_z) * n_y + y, s

    def sub_peer(d):
        return b, (s + d) % n_sub

    def remote(src, dst, k, peer):
        return pltpu.make_async_remote_copy(
            src_ref=src, dst_ref=dst, send_sem=send.at[k], recv_sem=recv.at[k], device_id=peer, device_id_type=MESH
        )

    def signal(sem, peer):
        pl.semaphore_signal(sem, inc=1, device_id=peer, device_id_type=MESH)

    ys, zs, ss = (sorted(range(1, n), key=lambda d: (-min(d, n - d), d)) for n in (n_y, n_z, n_sub))
    has_lower, has_upper = b > 0, b < n_branch - 1
    lower, upper = (b - 1, s), (b + 1, s)

    barrier = pltpu.get_barrier_semaphore()
    pl.when(has_lower)(lambda: signal(barrier, lower))
    pl.when(has_upper)(lambda: signal(barrier, upper))
    for d in ss:
        signal(barrier, sub_peer(d))
    for d in ys:
        signal(barrier, y_peer(d))
    for other in range(1, n_z):
        pl.when(other > z)(lambda other=other: signal(barrier, (other * n_y + y, s)))

    starts_late = z >= n_z // 2
    met = n_sub - 1 + n_y - 1 + z + has_lower.astype(jnp.int32) + has_upper.astype(jnp.int32)

    def along_z(ref, k, higher):
        for d in zs:
            pl.when(z + d < n_z if higher else z + d >= n_z)(
                lambda d=d: remote(ref.at[0], ref.at[d], k, z_peer(d)).start()
            )

    def enter():
        pl.semaphore_wait(barrier, met)
        for other in range(n_z - 1):
            pl.when(other < z)(lambda other=other: signal(later, (other * n_y + y, s)))
        l_sk1.wait()
        l_list1.wait()
        l_list2.wait()
        l_ntr.wait()
        row = [sk1[0, 0:1], sk1[0, 1:2], list1[...].astype(F32), list2[...].astype(F32)]
        row = jnp.concatenate(row + [jnp.zeros((1, 128 - 2 * RANK - 16), F32)], 1)
        info[0] = row
        early[0, 8:9] = row
        early[0, 0:8] = jnp.concatenate([ntr[0, 8 * k : 8 * (k + 1)] for k in range(4)], 1)
        for d in ys:
            remote(info.at[0], info.at[d], 4, y_peer(d)).start()
        along_z(early, 8, False)

    for copy in (l_vec, l_ntr, l_sk1, l_list1, l_list2, l_crd, l_sk2, l_near):
        copy.start()

    for side, missing in ((0, b == 0), (1, b == n_branch - 1)):

        @pl.when(missing)
        def _(side=side):
            hv[side] = jnp.zeros(hv.shape[1:], F32)
            hc[side] = jnp.zeros(hc.shape[1:], F32)

    l_ltr.wait()
    l_bas.wait()

    def make_w(i, c):
        cols = leaf_cols(i)
        bh, bl = split(bas[:, cols])
        lh, ll = split(ltr[i])
        w = dot_bf16(jnp.concatenate([lh, lh, ll], 0), jnp.concatenate([bh, bl, bh], 0), TN)
        wh, wl = split(w)
        w3[:RANK, cols] = wh
        w3[RANK : 2 * RANK, cols] = wl
        w3[2 * RANK :, cols] = wh
        return c

    lax.fori_loop(0, leaves, make_w, 0, unroll=16)

    l_vec.wait()

    def own_vectors(i, c):
        high, low = split(vec[:, leaf_cols(i)] * LN2)
        vw[RIM + i, :NV] = high
        vw[RIM + i, NV:] = low
        return c

    lax.fori_loop(0, leaves, own_vectors, 0, unroll=8)
    enters_first = starts_late & (y >= 2) & (y <= n_y - 2)
    pl.when(enters_first)(enter)
    own = jnp.concatenate([vw[RIM + i] for i in range(leaves)], 1)
    coeff_t = fold(dot_bf16(own, w3[: 2 * RANK], NT)) * (1.0 / LN2)
    coeff = coeff_t.T
    column[0] = jnp.concatenate([coeff[: RANK // 2], coeff[RANK // 2 :]], 1)
    pl.when(jnp.logical_not(enters_first))(enter)
    along_z(column, 5, False)

    rim = RIM * LEAF
    first, last = pl.ds(0, rim), pl.ds(leaves * LEAF - rim, rim)
    top, bottom = pl.ds(0, NV // 2), pl.ds(NV // 2, NV // 2)
    down = [
        remote(crd.at[:, first], hc.at[1], 0, lower),
        remote(vec.at[top, first], hv.at[1, top], 2, lower),
        remote(vec.at[bottom, first], hv.at[1, bottom], 9, lower),
    ]
    up = [
        remote(crd.at[:, last], hc.at[0], 1, upper),
        remote(vec.at[top, last], hv.at[0, top], 3, upper),
        remote(vec.at[bottom, last], hv.at[0, bottom], 10, upper),
    ]

    def start_all(copies):
        for copy in copies:
            copy.start()

    upper_early = has_upper & jnp.logical_not(starts_late & (y == n_y - 1))
    upper_late = has_upper & starts_late & (y == n_y - 1)

    l_crd.wait()
    pl.when(has_lower)(lambda: start_all(down))
    pl.when(upper_early)(lambda: start_all(up))
    wide = 8 * LEAF

    def own_features(i, c):
        cols = pl.ds(pl.multiple_of(i * wide, wide), wide)
        source, target = features(crd[:, cols])
        ft[:, cols] = target.astype(BF16)
        flat = source.T.astype(BF16)
        for k in range(8):
            fs[RIM + i * 8 + k] = flat[k * LEAF : (k + 1) * LEAF]
        return c

    lax.fori_loop(0, leaves // 8, own_features, 0)
    l_sk2.wait()
    sk2t[...] = jnp.concatenate([sk2[0].T, sk2[1].T], 1)

    def source_names(scale, offset):
        names = []
        for d in range(n_z):
            name = ((z + n_z - d) % n_z * n_y + y) * scale + offset
            names.append(jnp.full((1, RANK), name.astype(F32), F32))
        return jnp.concatenate(names, 1)

    def counted_tile(at, target, source, names, lane):
        sx = jnp.concatenate([r[:, :RANK] for r in source], 1) * SCALE
        sy = jnp.concatenate([r[:, RANK : 2 * RANK] for r in source], 1) * SCALE
        dx = at[:, 0:1] - sx
        dy = at[:, 1:2] - sy
        count = jnp.zeros((n_y, n_z * RANK), F32)
        for k in range(8):
            count = count + (target[:, lane + k : lane + k + 1] == names).astype(F32)
        count = jnp.concatenate([jnp.broadcast_to(count[d : d + 1], (RANK, n_z * RANK)) for d in range(n_y)], 0)
        return matern_of(dx * dx + dy * dy) * (count * LN2)

    def targets():
        return jnp.concatenate([info[(n_y - d) % n_y] for d in range(n_y)], 0)

    def keep_mix(level, tile):
        high, low = split(tile)
        mix[level * n_y * RANK : (level + 1) * n_y * RANK] = jnp.concatenate([high, high, low], 1)

    def prepare_groups():
        remote(info.at[ny1], info.at[ny1], 4, y_peer(1)).wait_recv()
        target = targets()
        group = [sk2t[pl.ds(z * n_y + (y + d) % n_y, 1)] for d in range(n_y)]
        line = [jnp.concatenate([target[d : d + 1, RANK * k : RANK * (k + 1)] for d in range(n_y)], 1) for k in range(2)]
        line += [jnp.concatenate([g[:, RANK * k : RANK * (k + 1)] for g in group], 1) for k in range(2)]
        at = (jnp.concatenate(line + [jnp.zeros((4, n_y * RANK), F32)], 0) * SCALE).T
        places[...] = at
        group_rows = [sk2t[pl.ds((z + n_z - d) % n_z * n_y + y, 1)] for d in range(n_z)]
        group_tile[...] = counted_tile(at[:, 2:4], target, group_rows, source_names(1, 0), 2 * RANK + 8)

    pl.when(z < n_z // 2)(prepare_groups)

    def send_higher():
        @pl.when(z < n_z - 1)
        def _():
            pl.semaphore_wait(later, n_z - 1 - z)

        along_z(early, 8, True)
        along_z(column, 5, True)

    in_second_half = z >= n_z // 2 - 1
    waits_less = b == 0
    parts_first = in_second_half | (y == n_y - 1)
    parts_step = jnp.where(parts_first, leaves // BLOCK, 1)
    group_step = jnp.where(parts_first | ((b == 0) & (s != 1)), 2, 3)
    pl.when(jnp.logical_not(waits_less))(send_higher)

    @pl.when(starts_late)
    def _():
        prepare_groups()
        pl.when(upper_late)(lambda: start_all(up))

    def prepare_nodes():
        remote(early.at[nz1], early.at[nz1], 8, z_peer(1)).wait_recv()
        moved = []
        for d in range(n_z):
            transfer = jnp.concatenate([early[d, 0:8, RANK * k : RANK * (k + 1)] for k in range(4)], 0)
            moved.append(dot_high(group_tile[:, d * RANK : (d + 1) * RANK], transfer, NT))
        keep_mix(1, jnp.concatenate(moved, 1))
        node_rows = [early[d, 8:9] for d in range(n_z)]
        keep_mix(0, counted_tile(places[:, 0:2], targets(), node_rows, source_names(n_sub, s), 2 * RANK))

    def send_level(level, own, theirs, k):
        coeffs = []
        for d in range(n_z):
            coeffs += [column[d, :, :NV], column[d, :, NV:]]
        high, low = split(jnp.concatenate(coeffs, 0))
        coeffs = jnp.concatenate([high, low, high], 0)
        fields = dot_bf16(mix[level * n_y * RANK : (level + 1) * n_y * RANK], coeffs)
        for d in [*ys, 0]:
            at = d * RANK
            own[d] = jnp.concatenate([fields[at : at + RANK // 2], fields[at + RANK // 2 : at + RANK]], 1)
            if d:
                remote(own.at[d], theirs.at[d], k, y_peer(d)).start()

    def send_parts():
        remote(column.at[nz1], column.at[nz1], 5, z_peer(1)).wait_recv()
        send_level(1, group_part, group_parts, 6)

    def send_nodes():
        send_level(0, node_part, node_parts, 11)

    def both_parts():
        prepare_nodes()
        send_parts()
        pl.when(jnp.logical_not(starts_late))(send_nodes)

    pl.when(parts_first)(both_parts)
    l_near.wait()

    def arrived(copies):
        for copy in copies:
            copy.wait_recv()

    def rims(waits, take):
        for side, there, copies in ((0, has_lower, up), (1, has_upper, down)):
            pl.when(there)(lambda copies=copies: arrived(copies[waits]))
            take(side, side * (RIM + leaves))

    def rim_features(side, base):
        source, _ = features(hc[side])
        flat = source.T.astype(BF16)
        for k in range(RIM):
            fs[base + k] = flat[k * LEAF : (k + 1) * LEAF]

    def rim_vectors(side, base):
        for i in range(RIM):
            high, low = split(hv[side, :, i * LEAF : (i + 1) * LEAF] * LN2)
            vw[base + i, :NV] = high
            vw[base + i, NV:] = low

    rims(slice(0, 1), rim_features)
    rims(slice(1, 3), rim_vectors)

    def near_leaves(first_leaf):
        items = [(first_leaf + u, pair) for u in range(BLOCK) for pair in PAIRS]

        def slots(i, pair):
            found = []
            for j in pair:
                named = near[j, i]
                slot = (named // (n_sub * leaves) - b) * leaves + named % leaves + RIM
                found.append(jnp.clip(slot, 0, leaves + 2 * RIM - 1))
            return found

        squares, tiles, acc = {}, {}, None
        for step in range(len(items) + 2):
            if step < len(items):
                i, pair = items[step]
                named = slots(i, pair)
                sources = jnp.concatenate([fs[m] for m in named], 0)
                squares[step] = named, dot_bf16(sources, ft[:, leaf_cols(i)])
            if 0 <= step - 1 < len(items):
                named, square = squares.pop(step - 1)
                tiles[step - 1] = named, jnp.concatenate(split(matern_of(square)), 1)
            if step >= 2:
                i, pair = items[step - 2]
                named, tile = tiles.pop(step - 2)
                part = dot_bf16(jnp.concatenate([vw[m] for m in named], 1), tile)
                acc = part if acc is None else acc + part
                if pair == PAIRS[-1]:
                    out[:, leaf_cols(i)] = fold(acc) + NUGGET * vec[:, leaf_cols(i)]
                    acc = None

    def send_group():
        remote(group_parts.at[ny1], group_parts.at[ny1], 6, y_peer(1)).wait_recv()
        field = group_part[0]
        for d in ys:
            field = field + group_parts[d]
        fc[0] = field
        for d in ss:
            remote(fc.at[0], fc.at[d], 7, sub_peer(d)).start()


    def near_block(t, c):
        pl.when((t == 1) & waits_less)(send_higher)
        pl.when(t == parts_step)(both_parts)
        pl.when((t == 1) & starts_late)(send_nodes)
        pl.when(t == group_step)(send_group)
        near_leaves(t * BLOCK)
        return c

    lax.fori_loop(0, leaves // BLOCK, near_block, 0)

    def finish(copies):
        for copy in copies:
            copy.wait_send()

    pl.when(has_lower)(lambda: finish(down))
    pl.when(has_upper)(lambda: finish(up))
    for ref, k in (
        (info.at[ny1], 4), (column.at[nz1], 5), (group_parts.at[ny1], 6), (fc.at[ns1], 7), (early.at[nz1], 8),
        (node_parts.at[ny1], 11),
    ):
        remote(ref, ref, k, sub_peer(1)).wait_send()

    remote(node_parts.at[ny1], node_parts.at[ny1], 11, y_peer(1)).wait_recv()
    field = node_part[0]
    for d in ys:
        field = field + node_parts[d]
    own_field = jnp.concatenate([field[:, :NV], field[:, NV:]], 0)
    remote(fc.at[ns1], fc.at[ns1], 7, sub_peer(1)).wait_recv()
    group = fc[0]
    for d in ss:
        group = group + fc[d]
    group = jnp.concatenate([group[:, :NV], group[:, NV:]], 0)
    field = own_field + dot_high(ntr[0], group)
    fh, fl = split(field.T)
    lhs = jnp.concatenate([fh, fh, fl], 1)

    for i in range(leaves // 2):
        cols = pl.ds(i * 2 * LEAF, 2 * LEAF)
        out[:, cols] += dot_bf16(lhs, w3[:, cols])


def body(sizes, vectors, coords, basis, leaf_transfer, node_transfer, skel_one, skel_two, near_list, list_one, list_two):
    n_branch, n_sub, n_y = sizes
    n_z = n_branch // n_y
    leaves = leaf_transfer.shape[0]
    window = leaves + 2 * RIM
    rim = RIM * LEAF
    operands = (
        vectors, coords, basis, leaf_transfer, node_transfer, skel_one,
        jnp.transpose(skel_two, (1, 2, 0)), near_list.T, list_one, list_two,
    )
    held = [pltpu.VMEM(a.shape, F32) for a in operands[:7]] + [pltpu.SMEM(operands[7].shape, jnp.int32)]
    held += [pltpu.VMEM(a.shape, jnp.int32) for a in operands[8:]]
    return pl.pallas_call(
        functools.partial(kernel, sizes),
        out_shape=pltpu.VMEM(vectors.shape, F32),
        in_specs=[pl.BlockSpec(memory_space=pltpu.HBM)] * 10,
        out_specs=pl.BlockSpec(memory_space=pltpu.VMEM),
        scratch_shapes=[
            *held,
            pltpu.VMEM((2, NV, rim), F32),
            pltpu.VMEM((2, 2, rim), F32),
            pltpu.VMEM((window, 2 * NV, LEAF), BF16),
            pltpu.VMEM((window, LEAF, FEATURES), BF16),
            pltpu.VMEM((FEATURES, leaves * LEAF), BF16),
            pltpu.VMEM((3 * RANK, leaves * LEAF), BF16),
            pltpu.VMEM((n_branch, 2 * RANK), F32),
            pltpu.VMEM((n_y, 1, 128), F32),
            pltpu.VMEM((n_z, 9, 128), F32),
            pltpu.VMEM((n_z, RANK // 2, 128), F32),
            pltpu.VMEM((n_y * RANK, 8), F32),
            pltpu.VMEM((n_y * RANK, n_z * RANK), F32),
            pltpu.VMEM((2 * n_y * RANK, 3 * n_z * RANK), BF16),
            pltpu.VMEM((n_y, RANK // 2, 128), F32),
            pltpu.VMEM((n_y, RANK // 2, 128), F32),
            pltpu.VMEM((n_y, RANK // 2, 128), F32),
            pltpu.VMEM((n_y, RANK // 2, 128), F32),
            pltpu.VMEM((n_sub, RANK // 2, 128), F32),
            pltpu.SemaphoreType.DMA((10,)),
            pltpu.SemaphoreType.DMA((12,)),
            pltpu.SemaphoreType.DMA((12,)),
            pltpu.SemaphoreType.REGULAR,
        ],
        compiler_params=pltpu.CompilerParams(
            collective_id=0, has_side_effects=True, vmem_limit_bytes=VMEM_LIMIT
        ),
        name="h2_product",
    )(*[pltpu.with_memory_space_constraint(a, pltpu.HBM) for a in operands])


def solution(mesh, y_count=Y_COUNT):
    both = ("branch", "sub")
    return jax.shard_map(
        functools.partial(body, (mesh.shape["branch"], mesh.shape["sub"], y_count)),
        mesh=mesh,
        in_specs=(
            P(None, both),
            P(None, both),
            P(None, both),
            P(both, None, None),
            P(both, None, None),
            P(both, None, None),
            P(),
            P(both, None),
            P(both, None),
            P("branch", None),
        ),
        out_specs=P(None, both),
        check_vma=False,
    )
```

```python
import functools
import math

import jax
import jax.numpy as jnp
from jax import lax
from jax.experimental import pallas as pl
from jax.experimental.pallas import tpu as pltpu
from jax.sharding import PartitionSpec as P

MESH = pl.DeviceIdType.MESH
F32 = jnp.float32
BF16 = jnp.bfloat16
NUGGET = 0.5
LOG2E = math.log2(math.e)
LN2 = math.log(2.0)
SCALE = math.sqrt(3.0) / 0.7 * LOG2E
Y_COUNT = 8
LEAF = 128
RANK = 32
NV = 64
RIM = 8
BLOCK = 8
PAIRS = ((0, 1), (2, 3), (4, 5), (6, 7), (8,))
EXACT = lax.Precision.HIGHEST
CENTRE = 1.5
VMEM_LIMIT = 48 * 2**20
FEATURES = 32
NN, NT, TN = ((1,), (0,)), ((1,), (1,)), ((0,), (0,))


def split(x):
    high = x.astype(BF16)
    return high, (x - high.astype(F32)).astype(BF16)


def split3(x):
    first = x.astype(BF16).astype(F32)
    rest = x - first
    second = rest.astype(BF16).astype(F32)
    return first, second, rest - second


def matern_of(square):
    square = jnp.maximum(square, 1e-30)
    dist = square * lax.rsqrt(square)
    return (dist + LOG2E) * jnp.exp2(-dist)


def features(coords):
    w = (coords - CENTRE) * SCALE
    norm = w[0:1] * w[0:1] + w[1:2] * w[1:2]
    s1, s2, s3 = split3(w)
    norms = split3(norm)
    ones = [jnp.ones_like(norm)] * 3
    zeros = jnp.zeros((FEATURES - 18, w.shape[1]), F32)
    t1, t2, t3 = -2.0 * s1, -2.0 * s2, -2.0 * s3
    source = jnp.concatenate([s1, s1, s2, s2, s1, s3, *norms, *ones, zeros], 0)
    target = jnp.concatenate([t1, t2, t1, t2, t3, t1, *ones, *norms, zeros], 0)
    return source, target


def dot_f32(a, b, dims=NN):
    return lax.dot_general(a, b, (dims, ((), ())), precision=EXACT, preferred_element_type=F32)


def dot_high(a, b, dims=NN):
    return lax.dot_general(a, b, (dims, ((), ())), precision=lax.Precision.HIGH, preferred_element_type=F32)


def dot_bf16(a, b, dims=NN):
    return lax.dot_general(a, b, (dims, ((), ())), preferred_element_type=F32)


def fold(r):
    half = r.shape[0] // 2, r.shape[1] // 2
    return r[: half[0], : half[1]] + r[half[0] :, : half[1]] + r[: half[0], half[1] :] + r[half[0] :, half[1] :]


def leaf_cols(i):
    return pl.ds(pl.multiple_of(i * LEAF, LEAF), LEAF)


def kernel(sizes, *refs):
    operands, out = refs[:10], refs[10]
    vec, crd, bas, ltr, ntr, sk1, sk2, near, list1, list2 = refs[11:21]
    hv, hc, vw, fs, ft, w3, sk2t, info, early, column, places, group_tile, mix, group_part, group_parts, node_part, node_parts, fc, load, send, recv, later = refs[21:]
    n_branch, n_sub, n_y = sizes
    n_z = n_branch // n_y
    leaves = ltr.shape[0]
    ny1, nz1, ns1 = pl.ds(1, n_y - 1), pl.ds(1, n_z - 1), pl.ds(1, n_sub - 1)
    b = lax.axis_index("branch")
    s = lax.axis_index("sub")
    z = b // n_y
    y = b % n_y

    loads = [pltpu.make_async_copy(operands[k], refs[11 + k], load.at[k]) for k in range(10)]
    l_vec, l_crd, l_bas, l_ltr, l_ntr, l_sk1, l_sk2, l_near, l_list1, l_list2 = loads
    l_ltr.start()
    l_bas.start()

    def y_peer(d):
        return z * n_y + (y + d) % n_y, s

    def z_peer(d):
        return ((z + d) % n_z) * n_y + y, s

    def sub_peer(d):
        return b, (s + d) % n_sub

    def remote(src, dst, k, peer):
        return pltpu.make_async_remote_copy(
            src_ref=src, dst_ref=dst, send_sem=send.at[k], recv_sem=recv.at[k], device_id=peer, device_id_type=MESH
        )

    def signal(sem, peer):
        pl.semaphore_signal(sem, inc=1, device_id=peer, device_id_type=MESH)

    ys, zs, ss = (sorted(range(1, n), key=lambda d: (-min(d, n - d), d)) for n in (n_y, n_z, n_sub))
    has_lower, has_upper = b > 0, b < n_branch - 1
    lower, upper = (b - 1, s), (b + 1, s)

    barrier = pltpu.get_barrier_semaphore()
    pl.when(has_lower)(lambda: signal(barrier, lower))
    pl.when(has_upper)(lambda: signal(barrier, upper))
    for d in ss:
        signal(barrier, sub_peer(d))
    for d in ys:
        signal(barrier, y_peer(d))
    for other in range(1, n_z):
        pl.when(other > z)(lambda other=other: signal(barrier, (other * n_y + y, s)))

    starts_late = z >= n_z // 2
    met = n_sub - 1 + n_y - 1 + z + has_lower.astype(jnp.int32) + has_upper.astype(jnp.int32)

    def along_z(ref, k, higher):
        for d in zs:
            pl.when(z + d < n_z if higher else z + d >= n_z)(
                lambda d=d: remote(ref.at[0], ref.at[d], k, z_peer(d)).start()
            )

    def enter():
        pl.semaphore_wait(barrier, met)
        for other in range(n_z - 1):
            pl.when(other < z)(lambda other=other: signal(later, (other * n_y + y, s)))
        l_sk1.wait()
        l_list1.wait()
        l_list2.wait()
        l_ntr.wait()
        row = [sk1[0, 0:1], sk1[0, 1:2], list1[...].astype(F32), list2[...].astype(F32)]
        row = jnp.concatenate(row + [jnp.zeros((1, 128 - 2 * RANK - 16), F32)], 1)
        info[0] = row
        early[0, 8:9] = row
        early[0, 0:8] = jnp.concatenate([ntr[0, 8 * k : 8 * (k + 1)] for k in range(4)], 1)
        for d in ys:
            remote(info.at[0], info.at[d], 4, y_peer(d)).start()
        along_z(early, 8, False)

    for copy in (l_vec, l_ntr, l_sk1, l_list1, l_list2, l_crd, l_sk2, l_near):
        copy.start()

    for side, missing in ((0, b == 0), (1, b == n_branch - 1)):

        @pl.when(missing)
        def _(side=side):
            hv[side] = jnp.zeros(hv.shape[1:], F32)
            hc[side] = jnp.zeros(hc.shape[1:], F32)

    l_ltr.wait()
    l_bas.wait()

    def make_w(i, c):
        cols = leaf_cols(i)
        bh, bl = split(bas[:, cols])
        lh, ll = split(ltr[i])
        w = dot_bf16(jnp.concatenate([lh, lh, ll], 0), jnp.concatenate([bh, bl, bh], 0), TN)
        wh, wl = split(w)
        w3[:RANK, cols] = wh
        w3[RANK : 2 * RANK, cols] = wl
        w3[2 * RANK :, cols] = wh
        return c

    lax.fori_loop(0, leaves, make_w, 0, unroll=16)

    l_vec.wait()

    def own_vectors(i, c):
        high, low = split(vec[:, leaf_cols(i)] * LN2)
        vw[RIM + i, :NV] = high
        vw[RIM + i, NV:] = low
        return c

    lax.fori_loop(0, leaves, own_vectors, 0, unroll=8)
    enters_first = starts_late & (y >= 2) & (y <= n_y - 2)
    pl.when(enters_first)(enter)
    own = jnp.concatenate([vw[RIM + i] for i in range(leaves)], 1)
    coeff_t = fold(dot_bf16(own, w3[: 2 * RANK], NT)) * (1.0 / LN2)
    coeff = coeff_t.T
    column[0] = jnp.concatenate([coeff[: RANK // 2], coeff[RANK // 2 :]], 1)
    pl.when(jnp.logical_not(enters_first))(enter)
    along_z(column, 5, False)

    rim = RIM * LEAF
    first, last = pl.ds(0, rim), pl.ds(leaves * LEAF - rim, rim)
    top, bottom = pl.ds(0, NV // 2), pl.ds(NV // 2, NV // 2)
    down = [
        remote(crd.at[:, first], hc.at[1], 0, lower),
        remote(vec.at[top, first], hv.at[1, top], 2, lower),
        remote(vec.at[bottom, first], hv.at[1, bottom], 9, lower),
    ]
    up = [
        remote(crd.at[:, last], hc.at[0], 1, upper),
        remote(vec.at[top, last], hv.at[0, top], 3, upper),
        remote(vec.at[bottom, last], hv.at[0, bottom], 10, upper),
    ]

    def start_all(copies):
        for copy in copies:
            copy.start()

    upper_early = has_upper & jnp.logical_not(starts_late & (y == n_y - 1))
    upper_late = has_upper & starts_late & (y == n_y - 1)

    l_crd.wait()
    pl.when(has_lower)(lambda: start_all(down))
    pl.when(upper_early)(lambda: start_all(up))
    wide = 8 * LEAF

    def own_features(i, c):
        cols = pl.ds(pl.multiple_of(i * wide, wide), wide)
        source, target = features(crd[:, cols])
        ft[:, cols] = target.astype(BF16)
        flat = source.T.astype(BF16)
        for k in range(8):
            fs[RIM + i * 8 + k] = flat[k * LEAF : (k + 1) * LEAF]
        return c

    lax.fori_loop(0, leaves // 8, own_features, 0)
    l_sk2.wait()
    sk2t[...] = jnp.concatenate([sk2[0].T, sk2[1].T], 1)

    def source_names(scale, offset):
        names = []
        for d in range(n_z):
            name = ((z + n_z - d) % n_z * n_y + y) * scale + offset
            names.append(jnp.full((1, RANK), name.astype(F32), F32))
        return jnp.concatenate(names, 1)

    def counted_tile(at, target, source, names, lane):
        sx = jnp.concatenate([r[:, :RANK] for r in source], 1) * SCALE
        sy = jnp.concatenate([r[:, RANK : 2 * RANK] for r in source], 1) * SCALE
        dx = at[:, 0:1] - sx
        dy = at[:, 1:2] - sy
        count = jnp.zeros((n_y, n_z * RANK), F32)
        for k in range(8):
            count = count + (target[:, lane + k : lane + k + 1] == names).astype(F32)
        count = jnp.concatenate([jnp.broadcast_to(count[d : d + 1], (RANK, n_z * RANK)) for d in range(n_y)], 0)
        return matern_of(dx * dx + dy * dy) * (count * LN2)

    def targets():
        return jnp.concatenate([info[(n_y - d) % n_y] for d in range(n_y)], 0)

    def keep_mix(level, tile):
        high, low = split(tile)
        mix[level * n_y * RANK : (level + 1) * n_y * RANK] = jnp.concatenate([high, high, low], 1)

    def prepare_groups():
        remote(info.at[ny1], info.at[ny1], 4, y_peer(1)).wait_recv()
        target = targets()
        group = [sk2t[pl.ds(z * n_y + (y + d) % n_y, 1)] for d in range(n_y)]
        line = [jnp.concatenate([target[d : d + 1, RANK * k : RANK * (k + 1)] for d in range(n_y)], 1) for k in range(2)]
        line += [jnp.concatenate([g[:, RANK * k : RANK * (k + 1)] for g in group], 1) for k in range(2)]
        at = (jnp.concatenate(line + [jnp.zeros((4, n_y * RANK), F32)], 0) * SCALE).T
        places[...] = at
        group_rows = [sk2t[pl.ds((z + n_z - d) % n_z * n_y + y, 1)] for d in range(n_z)]
        group_tile[...] = counted_tile(at[:, 2:4], target, group_rows, source_names(1, 0), 2 * RANK + 8)

    pl.when(z < n_z // 2)(prepare_groups)

    def send_higher():
        @pl.when(z < n_z - 1)
        def _():
            pl.semaphore_wait(later, n_z - 1 - z)

        along_z(early, 8, True)
        along_z(column, 5, True)

    in_second_half = z >= n_z // 2 - 1
    waits_less = b == 0
    parts_first = in_second_half | (y == n_y - 1)
    parts_step = jnp.where(parts_first, leaves // BLOCK, 1)
    group_step = jnp.where(parts_first | ((b == 0) & (s != 1)), 2, 3)
    pl.when(jnp.logical_not(waits_less))(send_higher)

    @pl.when(starts_late)
    def _():
        prepare_groups()
        pl.when(upper_late)(lambda: start_all(up))

    def prepare_nodes():
        remote(early.at[nz1], early.at[nz1], 8, z_peer(1)).wait_recv()
        moved = []
        for d in range(n_z):
            transfer = jnp.concatenate([early[d, 0:8, RANK * k : RANK * (k + 1)] for k in range(4)], 0)
            moved.append(dot_high(group_tile[:, d * RANK : (d + 1) * RANK], transfer, NT))
        keep_mix(1, jnp.concatenate(moved, 1))
        node_rows = [early[d, 8:9] for d in range(n_z)]
        keep_mix(0, counted_tile(places[:, 0:2], targets(), node_rows, source_names(n_sub, s), 2 * RANK))

    def send_level(level, own, theirs, k):
        coeffs = []
        for d in range(n_z):
            coeffs += [column[d, :, :NV], column[d, :, NV:]]
        high, low = split(jnp.concatenate(coeffs, 0))
        coeffs = jnp.concatenate([high, low, high], 0)
        fields = dot_bf16(mix[level * n_y * RANK : (level + 1) * n_y * RANK], coeffs)
        for d in [*ys, 0]:
            at = d * RANK
            own[d] = jnp.concatenate([fields[at : at + RANK // 2], fields[at + RANK // 2 : at + RANK]], 1)
            if d:
                remote(own.at[d], theirs.at[d], k, y_peer(d)).start()

    def send_parts():
        remote(column.at[nz1], column.at[nz1], 5, z_peer(1)).wait_recv()
        send_level(1, group_part, group_parts, 6)

    nodes_later = starts_late & (y > 0)

    def send_nodes():
        send_level(0, node_part, node_parts, 11)

    def both_parts():
        prepare_nodes()
        send_parts()
        pl.when(jnp.logical_not(nodes_later))(send_nodes)

    pl.when(parts_first)(both_parts)
    l_near.wait()

    def arrived(copies):
        for copy in copies:
            copy.wait_recv()

    def rims(waits, take):
        for side, there, copies in ((0, has_lower, up), (1, has_upper, down)):
            pl.when(there)(lambda copies=copies: arrived(copies[waits]))
            take(side, side * (RIM + leaves))

    def rim_features(side, base):
        source, _ = features(hc[side])
        flat = source.T.astype(BF16)
        for k in range(RIM):
            fs[base + k] = flat[k * LEAF : (k + 1) * LEAF]

    def rim_vectors(side, base):
        for i in range(RIM):
            high, low = split(hv[side, :, i * LEAF : (i + 1) * LEAF] * LN2)
            vw[base + i, :NV] = high
            vw[base + i, NV:] = low

    rims(slice(0, 1), rim_features)
    rims(slice(1, 3), rim_vectors)

    def near_leaves(first_leaf):
        items = [(first_leaf + u, pair) for u in range(BLOCK) for pair in PAIRS]

        def slots(i, pair):
            found = []
            for j in pair:
                named = near[j, i]
                slot = (named // (n_sub * leaves) - b) * leaves + named % leaves + RIM
                found.append(jnp.clip(slot, 0, leaves + 2 * RIM - 1))
            return found

        squares, tiles, acc = {}, {}, None
        for step in range(len(items) + 2):
            if step < len(items):
                i, pair = items[step]
                named = slots(i, pair)
                sources = jnp.concatenate([fs[m] for m in named], 0)
                squares[step] = named, dot_bf16(sources, ft[:, leaf_cols(i)])
            if 0 <= step - 1 < len(items):
                named, square = squares.pop(step - 1)
                tiles[step - 1] = named, jnp.concatenate(split(matern_of(square)), 1)
            if step >= 2:
                i, pair = items[step - 2]
                named, tile = tiles.pop(step - 2)
                part = dot_bf16(jnp.concatenate([vw[m] for m in named], 1), tile)
                acc = part if acc is None else acc + part
                if pair == PAIRS[-1]:
                    out[:, leaf_cols(i)] = fold(acc) + NUGGET * vec[:, leaf_cols(i)]
                    acc = None

    def send_group():
        remote(group_parts.at[ny1], group_parts.at[ny1], 6, y_peer(1)).wait_recv()
        field = group_part[0]
        for d in ys:
            field = field + group_parts[d]
        fc[0] = field
        for d in ss:
            remote(fc.at[0], fc.at[d], 7, sub_peer(d)).start()


    def near_block(t, c):
        pl.when((t == 1) & waits_less)(send_higher)
        pl.when(t == parts_step)(both_parts)
        pl.when((t == 1) & nodes_later)(send_nodes)
        pl.when(t == group_step)(send_group)
        near_leaves(t * BLOCK)
        return c

    lax.fori_loop(0, leaves // BLOCK, near_block, 0)

    def finish(copies):
        for copy in copies:
            copy.wait_send()

    pl.when(has_lower)(lambda: finish(down))
    pl.when(has_upper)(lambda: finish(up))
    for ref, k in (
        (info.at[ny1], 4), (column.at[nz1], 5), (group_parts.at[ny1], 6), (fc.at[ns1], 7), (early.at[nz1], 8),
        (node_parts.at[ny1], 11),
    ):
        remote(ref, ref, k, sub_peer(1)).wait_send()

    remote(node_parts.at[ny1], node_parts.at[ny1], 11, y_peer(1)).wait_recv()
    field = node_part[0]
    for d in ys:
        field = field + node_parts[d]
    own_field = jnp.concatenate([field[:, :NV], field[:, NV:]], 0)
    remote(fc.at[ns1], fc.at[ns1], 7, sub_peer(1)).wait_recv()
    group = fc[0]
    for d in ss:
        group = group + fc[d]
    group = jnp.concatenate([group[:, :NV], group[:, NV:]], 0)
    field = own_field + dot_high(ntr[0], group)
    fh, fl = split(field.T)
    lhs = jnp.concatenate([fh, fh, fl], 1)

    for i in range(leaves // 2):
        cols = pl.ds(i * 2 * LEAF, 2 * LEAF)
        out[:, cols] += dot_bf16(lhs, w3[:, cols])


def body(sizes, vectors, coords, basis, leaf_transfer, node_transfer, skel_one, skel_two, near_list, list_one, list_two):
    n_branch, n_sub, n_y = sizes
    n_z = n_branch // n_y
    leaves = leaf_transfer.shape[0]
    window = leaves + 2 * RIM
    rim = RIM * LEAF
    operands = (
        vectors, coords, basis, leaf_transfer, node_transfer, skel_one,
        jnp.transpose(skel_two, (1, 2, 0)), near_list.T, list_one, list_two,
    )
    held = [pltpu.VMEM(a.shape, F32) for a in operands[:7]] + [pltpu.SMEM(operands[7].shape, jnp.int32)]
    held += [pltpu.VMEM(a.shape, jnp.int32) for a in operands[8:]]
    return pl.pallas_call(
        functools.partial(kernel, sizes),
        out_shape=pltpu.VMEM(vectors.shape, F32),
        in_specs=[pl.BlockSpec(memory_space=pltpu.HBM)] * 10,
        out_specs=pl.BlockSpec(memory_space=pltpu.VMEM),
        scratch_shapes=[
            *held,
            pltpu.VMEM((2, NV, rim), F32),
            pltpu.VMEM((2, 2, rim), F32),
            pltpu.VMEM((window, 2 * NV, LEAF), BF16),
            pltpu.VMEM((window, LEAF, FEATURES), BF16),
            pltpu.VMEM((FEATURES, leaves * LEAF), BF16),
            pltpu.VMEM((3 * RANK, leaves * LEAF), BF16),
            pltpu.VMEM((n_branch, 2 * RANK), F32),
            pltpu.VMEM((n_y, 1, 128), F32),
            pltpu.VMEM((n_z, 9, 128), F32),
            pltpu.VMEM((n_z, RANK // 2, 128), F32),
            pltpu.VMEM((n_y * RANK, 8), F32),
            pltpu.VMEM((n_y * RANK, n_z * RANK), F32),
            pltpu.VMEM((2 * n_y * RANK, 3 * n_z * RANK), BF16),
            pltpu.VMEM((n_y, RANK // 2, 128), F32),
            pltpu.VMEM((n_y, RANK // 2, 128), F32),
            pltpu.VMEM((n_y, RANK // 2, 128), F32),
            pltpu.VMEM((n_y, RANK // 2, 128), F32),
            pltpu.VMEM((n_sub, RANK // 2, 128), F32),
            pltpu.SemaphoreType.DMA((10,)),
            pltpu.SemaphoreType.DMA((12,)),
            pltpu.SemaphoreType.DMA((12,)),
            pltpu.SemaphoreType.REGULAR,
        ],
        compiler_params=pltpu.CompilerParams(
            collective_id=0, has_side_effects=True, vmem_limit_bytes=VMEM_LIMIT
        ),
        name="h2_product",
    )(*[pltpu.with_memory_space_constraint(a, pltpu.HBM) for a in operands])


def solution(mesh, y_count=Y_COUNT):
    both = ("branch", "sub")
    return jax.shard_map(
        functools.partial(body, (mesh.shape["branch"], mesh.shape["sub"], y_count)),
        mesh=mesh,
        in_specs=(
            P(None, both),
            P(None, both),
            P(None, both),
            P(both, None, None),
            P(both, None, None),
            P(both, None, None),
            P(),
            P(both, None),
            P(both, None),
            P("branch", None),
        ),
        out_specs=P(None, both),
        check_vma=False,
    )
```
